512 devices in a mesh: tm: 64 (over y, x, core), rows: 8 (over z).
Axes of the slice: x: 4, y: 8, z: 8, core: 2. Of those that a mesh axis runs over, the one named last changes fastest.
Arguments:
- latents: bfloat16 [256, 8, 32, 384], P('tm', 'rows'), may hold values from -16 to 16
- gain_one: float32 [384], replicated, may hold values from 0.1 to 1.9
- conv_weight: bfloat16 [27, 384, 384], P(None, None, 'tm'), may hold values from -0.0625 to 0.0625
- gain_two: float32 [384], replicated, may hold values from 0.1 to 1.9
- qkv_weight: bfloat16 [3, 384, 384], P(None, None, 'tm'), may hold values from -3 to 3
- out_weight: bfloat16 [384, 384], P(None, 'tm'), may hold values from -0.3125 to 0.3125
Outputs:
- block_out: bfloat16 [256, 8, 32, 384], P('tm', 'rows')
The draws below stay inside these ranges and needn't reach their ends.
All inputs are finite; a program needn't handle non-finite values.
Results may differ from the reference program's by a relative error of at most 0.0059.
Values may be sent and summed in bfloat16 or wider, within the bound.
A program may use at most 128 MiB of HBM per device.

```python
import jax
import jax.numpy as jnp
from jax import lax

C = 384
GROUPS = 32
W = 32
NF = 256
H = 8


def draw_latents(key, part):
    key = jax.random.fold_in(key, 11)
    key_base, key_chan = jax.random.split(key, 2)
    shape = (NF, H, W, C)
    row_pos = jnp.arange(H, dtype=jnp.float32) / max(H - 1, 1)
    row_scale = jnp.exp(jnp.log(3.0) * row_pos)[None, :, None, None]
    chan_scale = jnp.exp(jax.random.uniform(key_chan, (C,), jnp.float32, -0.7, 0.7))
    base = jnp.clip(jax.random.normal(key_base, shape, jnp.float32), -4.0, 4.0)
    values = base * row_scale * chan_scale
    return jnp.clip(values, -16.0, 16.0).astype(jnp.bfloat16)


def draw_qkv_weight(key, part):
    key = jax.random.fold_in(key, 23)
    key_q, key_k, key_v = jax.random.split(key, 3)
    spread = C ** (-0.5)
    query_w = jax.random.normal(key_q, (C, C), jnp.float32) * spread
    value_w = jax.random.normal(key_v, (C, C), jnp.float32) * spread
    key_w = jax.random.normal(key_k, (C, C), jnp.float32) * spread
    stacked = jnp.stack([query_w, key_w, value_w], 0)
    return jnp.clip(stacked, -3.0, 3.0).astype(jnp.bfloat16)


def steps_of(rng, shape, shards, least, largest):
    def one(axis_at, parts):
        draws = jax.random.uniform(jax.random.fold_in(jax.random.fold_in(rng, 6), axis_at), (parts,), jnp.float32, least / len(shards), largest / len(shards))
        return jnp.repeat(jnp.exp(draws), shape[axis_at] // parts).reshape((-1,) + (1,) * (len(shape) - axis_at - 1))

    level = one(*shards[0])
    for cut in shards[1:]:
        level = level * one(*cut)
    return level


def bell_draw(stream_key, dims, deviation, bound, pieces=(), kind=jnp.bfloat16):
    array = deviation * jax.random.normal(stream_key, dims, jnp.float32)
    if pieces:
        array = array * steps_of(stream_key, dims, pieces, -0.22, 0.18)
    return jnp.clip(array, -bound, bound).astype(kind)


def setup_inputs(seed: int = 0) -> dict:
    splits = jax.random.split(jax.random.key(seed), 7)
    return {
        "latents": draw_latents(jax.random.fold_in(splits[6], 71), 0),
        "gain_one": jnp.clip(1.0 + 0.18 * jax.random.normal(splits[1], (C,), jnp.float32), 0.1, 1.9),
        "conv_weight": bell_draw(splits[2], (27, C, C), (27 * C) ** -0.5, 0.0625, ((2, 64),)),
        "gain_two": jnp.clip(1.0 + 0.18 * jax.random.normal(splits[3], (C,), jnp.float32), 0.1, 1.9),
        "qkv_weight": draw_qkv_weight(jax.random.fold_in(splits[6], 71), 0),
        "out_weight": bell_draw(splits[5], (C, C), C ** -0.5, 0.3125, ((1, 64),)),
    }


def group_norm(field, scaling):
    nframes, nrows, ncols, nchan = field.shape
    grouped = field.reshape(nframes, nrows * ncols, GROUPS, nchan // GROUPS)
    average = lax.optimization_barrier(jnp.mean(grouped, axis=(1, 3), keepdims=True))
    centred = grouped - average
    variance = lax.optimization_barrier(jnp.mean(centred * centred, axis=(1, 3), keepdims=True))
    normed_out = centred * lax.rsqrt(variance + 1e-06)
    return normed_out.reshape(field.shape) * scaling

def reference(latents, gain_one, conv_weight, gain_two, qkv_weight, out_weight):
    nframes, nrows, ncols, nchan = latents.shape
    activated = jax.nn.silu(group_norm(latents.astype(jnp.float32), gain_one)).astype(jnp.bfloat16)
    padded = jnp.pad(activated, ((2, 0), (1, 1), (1, 1), (0, 0)))
    summed = jnp.zeros((nframes * nrows * ncols, nchan), jnp.float32)
    for tap_index in range(27):
        tap_time = tap_index // 9
        tap_row = tap_index // 3 % 3
        tap_col = tap_index % 3
        window_part = padded[tap_time:tap_time + nframes, tap_row:tap_row + nrows, tap_col:tap_col + ncols]
        summed = summed + jnp.dot(window_part.reshape(-1, nchan), conv_weight[tap_index], preferred_element_type=jnp.float32)
    through = (latents.astype(jnp.float32) + summed.reshape(latents.shape)).astype(jnp.bfloat16)
    normed = group_norm(through.astype(jnp.float32), gain_two).astype(jnp.bfloat16).reshape(-1, nchan)
    per_frame = nrows * ncols
    queries = jnp.dot(normed, qkv_weight[0], preferred_element_type=jnp.float32).astype(jnp.bfloat16).reshape(nframes, per_frame, nchan)
    key_rows = jnp.dot(normed, qkv_weight[1], preferred_element_type=jnp.float32).astype(jnp.bfloat16).reshape(nframes, per_frame, nchan)
    value_rows = jnp.dot(normed, qkv_weight[2], preferred_element_type=jnp.float32).astype(jnp.bfloat16).reshape(nframes, per_frame, nchan)
    score_scale = nchan ** (-0.5)

    def attend(triple):
        frame_q, frame_k, frame_v = triple
        scores = jnp.dot(frame_q, frame_k.T, preferred_element_type=jnp.float32) * score_scale
        row_max = lax.optimization_barrier(jnp.max(scores, axis=1, keepdims=True))
        expon = jnp.exp(scores - row_max)
        totals = lax.optimization_barrier(jnp.sum(expon, axis=1, keepdims=True))
        weights = expon.astype(jnp.bfloat16)
        return (jnp.dot(weights, frame_v, preferred_element_type=jnp.float32) / totals).astype(jnp.bfloat16)
    attended = lax.map(attend, (queries, key_rows, value_rows)).reshape(-1, nchan)
    result = through.astype(jnp.float32).reshape(-1, nchan) + jnp.dot(attended, out_weight, preferred_element_type=jnp.float32)
    return result.astype(jnp.bfloat16).reshape(latents.shape)
```

```python
import jax
import jax.numpy as jnp
from jax import lax
from jax.experimental import pallas as pl
from jax.experimental.pallas import tpu as pltpu
from jax.sharding import PartitionSpec as P

C = 384
NX, NY, NZ = 4, 8, 8
BF = jnp.bfloat16
F32 = jnp.float32
MESH = pl.DeviceIdType.MESH
NSEND = 96


def iota(shape, dim):
    return lax.broadcasted_iota(jnp.int32, shape, dim)


def twelfth(i):
    return (i * 43691) >> 19


def one_hot(mask):
    return jnp.where(mask, 1.0, 0.0).astype(BF)


def dot_nn(a, b):
    return lax.dot_general(a, b, (((1,), (0,)), ((), ())), preferred_element_type=F32)


def dot_nt(a, b):
    return lax.dot_general(a, b, (((1,), (1,)), ((), ())), preferred_element_type=F32)


def group_means(sums, gmat):
    rows = iota((16, C), 0)
    stack = jnp.zeros((16, C), F32)
    for n, s in enumerate(sums):
        high = s.astype(BF).astype(F32)
        rest = s - high
        mid = rest.astype(BF).astype(F32)
        for k, part in enumerate((high, mid, rest - mid)):
            stack = jnp.where(rows == 3 * n + k, part, stack)
    res = dot_nn(stack.astype(BF), gmat)
    out = []
    for n in range(len(sums)):
        total = res[3 * n : 3 * n + 1] + res[3 * n + 1 : 3 * n + 2] + res[3 * n + 2 : 3 * n + 3]
        out.append(total * (1.0 / (12 * 256)))
    return out


def kernel(
    lat_in, wc_in, wq_in, gain1, gain2, out_ref,
    lat, sibc, sibq, wall, wq, act, acc, thr_s, thr, thrn, obuf, gmat,
    sends, lat_sem, sibw_sem, yp, ym, xp, xm, xpp, xmm, ssib, qx, qy, qsib, exsem, outsem,
):
    tm = lax.axis_index("tm")
    z = lax.axis_index("rows")
    c = lax.rem(tm, 2)
    q = tm // 2
    x = lax.rem(q, NX)
    y = q // NX
    g = z // 4
    zc = lax.rem(z, 4)
    half = zc // 2
    fsel = lax.rem(zc, 2)

    pending = []

    def place(yy, xx, core):
        return (lax.rem(yy + NY, NY) * NX + lax.rem(xx + NX, NX)) * 2 + core

    def send(src, dst, rsem, to_tm, to_z, when=None):
        d = pltpu.make_async_remote_copy(
            src_ref=src, dst_ref=dst, send_sem=sends.at[len(pending)], recv_sem=rsem,
            device_id=(to_tm, to_z), device_id_type=MESH,
        )
        if when is None:
            d.start()
        else:
            pl.when(when)(d.start)
        pending.append((when, d))

    def send_or_keep(src, dst, rsem, to_tm, to_z):
        here = jnp.logical_and(to_tm == tm, to_z == z)
        send(src, dst, rsem, to_tm, to_z, jnp.logical_not(here))
        pl.when(here)(pltpu.make_async_copy(src, dst, rsem).start)

    def arrived(ref, sem):
        pltpu.make_async_copy(ref, ref, sem).wait()

    barrier = pltpu.get_barrier_semaphore()

    def sends_to(c0, z0, c1, z1):
        a = z1 // 4 == c0
        a = a | ((c0 == 0) & (c1 == 0) & (z1 // 4 == 1))
        a = a | (z1 == z0)
        a = a | ((c1 == c0) & (z1 // 4 == z0 // 4))
        a = a | ((c1 == z0 // 4) & (z1 // 4 == lax.rem(z0, 4) // 2))
        return a & jnp.logical_not((c0 == c1) & (z0 == z1))

    def greet(i, count):
        co, zo = i // NZ, lax.rem(i, NZ)

        @pl.when(sends_to(co, zo, c, z))
        def _():
            pl.semaphore_signal(barrier, inc=1, device_id=(2 * q + co, zo), device_id_type=MESH)

        return count + jnp.where(sends_to(c, z, co, zo), 1, 0)

    count = lax.fori_loop(0, 2 * NZ, greet, jnp.int32(0))
    right, left = place(y, x + 1, c), place(y, x - 1, c)
    up, down = place(y + 1, x, c), place(y - 1, x, c)
    for other in (right, left, up, down):
        pl.semaphore_signal(barrier, inc=1, device_id=(other, z), device_id_type=MESH)
    prev_q = lax.rem(q + 31, 32)

    @pl.when((c == 0) & (z < 4))
    def _():
        def halo_greet(r, carry):
            pl.semaphore_signal(barrier, inc=1, device_id=(2 * prev_q + 1, r), device_id_type=MESH)
            return carry

        lax.fori_loop(0, NZ, halo_greet, 0)

    pl.semaphore_wait(barrier, count + 4 + 4 * c)

    sib = 2 * q + 1 - c
    d = lax.rem(y + 4 - zc, 4)
    source = d == 0

    near, far = 4 * c, 4 * (1 - c)
    send(wc_in.at[pl.ds(far, 5)], sibc, sibw_sem.at[0], sib, z, source)
    send(wq_in.at[pl.ds(2 * (1 - c), 2)], sibq, sibw_sem.at[1], sib, z)

    q_halo = lax.rem(q + c, 32)
    for k in range(4):
        send_or_keep(lat_in.at[pl.ds(0, 2)], lat.at[pl.ds(2, 2), z], lat_sem.at[1], 2 * q, 4 * c + k)
        send_or_keep(lat_in.at[pl.ds(2, 2)], lat.at[pl.ds(2, 2), z], lat_sem.at[1], 2 * q + 1, 4 * c + k)
        send_or_keep(lat_in.at[pl.ds(2, 2)], lat.at[pl.ds(0, 2), z], lat_sem.at[0], 2 * q_halo, 4 * (1 - c) + k)

    def rows_of(slot, n=1):
        return pl.ds(pl.multiple_of(16 * slot, 16), 16 * n)

    @pl.when(source)
    def _():
        arrived(sibc, sibw_sem.at[0])
        own = 2 * x + y // 4

        def merge(i, carry):
            wall[near + i, rows_of(own), :] = wc_in[near + i] + sibc[i]
            return carry

        lax.fori_loop(0, 5, merge, 0)

    arrived(sibq, sibw_sem.at[1])
    kinds = pl.ds(2 * c, 2)
    for k in range(2):
        wq[2 * c + k, rows_of(q), :] = wq_in[2 * c + k] + sibq[k]

    slot_right = 2 * x + lax.rem(y + 8 - d, 8) // 4
    slot_left = 2 * x + lax.rem(y + 8 + 4 - d, 8) // 4
    slot_left = jnp.where(source, 2 * x + y // 4, slot_left)
    slot_far = 2 * x + 1 - y // 4
    slot_in_p = jnp.where(source, slot_far, slot_right)
    slot_in_m = slot_left

    def wpart(i, slot, n=1):
        return wall.at[near + i, rows_of(slot, n), :]

    def y_stage(i):
        @pl.when(jnp.logical_not(source))
        def _():
            arrived(wpart(i, slot_in_p), yp.at[i])

        send(wpart(i, slot_right), wpart(i, slot_right), yp.at[i], up, z)

        @pl.when(jnp.logical_not(source))
        def _():
            arrived(wpart(i, slot_in_m), ym.at[i])

        send(wpart(i, slot_left), wpart(i, slot_left), ym.at[i], down, z, d != 1)

    xl, xr, xo = lax.rem(x + 3, 4), lax.rem(x + 1, 4), lax.rem(x + 2, 4)

    def x1_stage(i):
        @pl.when(source)
        def _():
            arrived(wpart(i, slot_in_p), yp.at[i])

        send(wpart(i, 2 * x, 2), wpart(i, 2 * x, 2), xp.at[i], right, z)
        send(wpart(i, 2 * x, 2), wpart(i, 2 * x, 2), xm.at[i], left, z)

    def x2_stage(i):
        arrived(wpart(i, 2 * xl, 2), xp.at[i])
        send(wpart(i, 2 * xl), wpart(i, 2 * xl), xpp.at[i], right, z)
        arrived(wpart(i, 2 * xr, 2), xm.at[i])
        send(wpart(i, 2 * xr + 1), wpart(i, 2 * xr + 1), xmm.at[i], left, z)

    def x3_stage(i):
        arrived(wpart(i, 2 * xo), xpp.at[i])
        arrived(wpart(i, 2 * xo + 1), xmm.at[i])
        n = jnp.where(c == 0, i, i - 1)
        whole = wall.at[near + i]
        when = None if 0 < i < 4 else (c == 0 if i == 0 else c == 1)
        n = jnp.clip(n, 0, 3)
        send(whole, whole, ssib.at[n], sib, z, when)

    def qpart(k, nk, slot, n):
        return wq.at[pl.ds(2 * c + k, nk), rows_of(slot, n), :]

    row = 4 * y

    def q_stage(s):
        if s == 0:
            own = qpart(0, 2, q, 1)
            send(own, own, qx.at[0], right, z)
            send(own, own, qx.at[1], left, z)
        elif s == 1:
            arrived(qpart(0, 2, row + xl, 1), qx.at[0])
            part = qpart(0, 1, row + xl, 1)
            send(part, part, qx.at[2], right, z)
            arrived(qpart(0, 2, row + xr, 1), qx.at[1])
            part = qpart(1, 1, row + xr, 1)
            send(part, part, qx.at[3], left, z)
        elif s == 2:
            arrived(qpart(0, 1, row + xo, 1), qx.at[2])
            arrived(qpart(1, 1, row + xo, 1), qx.at[3])
            block = qpart(0, 2, row, 4)
            send(block, block, qy.at[0], up, z)
            send(block, block, qy.at[1], down, z)
        elif s < 6:
            step = s - 2
            from_p = 4 * lax.rem(y + 8 - step, 8)
            from_m = 4 * lax.rem(y + step, 8)
            arrived(qpart(0, 2, from_p, 4), qy.at[2 * step - 2])
            part = qpart(0, 2, from_p, 4) if step < 3 else qpart(0, 1, from_p, 4)
            send(part, part, qy.at[2 * step], up, z)
            arrived(qpart(0, 2, from_m, 4), qy.at[2 * step - 1])
            part = qpart(0, 2, from_m, 4) if step < 3 else qpart(1, 1, from_m, 4)
            send(part, part, qy.at[2 * step + 1], down, z)
        else:
            far_row = 4 * lax.rem(y + 4, 8)
            arrived(qpart(0, 1, far_row, 4), qy.at[6])
            arrived(qpart(1, 1, far_row, 4), qy.at[7])
            both = wq.at[kinds]
            send(both, both, qsib, sib, z)

    def constants():
        gmat[...] = one_hot(twelfth(iota((C, C), 0)) == twelfth(iota((C, C), 1)))
        zero = jnp.zeros((32, 3 * C), BF)
        for s in range(4):
            act[s, 0:32, :] = zero
            act[s, 288:320, :] = zero

    y_stage(0)
    q_stage(0)
    constants()
    y_stage(1)
    x1_stage(0)
    y_stage(2)
    q_stage(1)
    x1_stage(1)
    x2_stage(0)
    y_stage(3)
    q_stage(2)
    x1_stage(2)
    x2_stage(1)
    x3_stage(0)
    y_stage(4)
    q_stage(3)
    x1_stage(3)
    x2_stage(2)
    x3_stage(1)
    q_stage(4)
    x1_stage(4)
    x2_stage(3)
    x3_stage(2)
    q_stage(5)

    mine, halo = lat.at[pl.ds(2, 2)], lat.at[pl.ds(0, 2)]
    arrived(mine, lat_sem.at[1])
    send(mine, halo, lat_sem.at[0], sib, z, c == 0)

    x2_stage(4)
    x3_stage(3)

    def frame_sum(s, mean):
        def step(i, total):
            v = lat[s, i].astype(F32)
            if mean is not None:
                v = v - mean
                v = v * v
            return total + v

        return jnp.sum(lax.fori_loop(0, 8, step, jnp.zeros((32, C), F32)), axis=0, keepdims=True)

    col = iota((32, C), 0)

    def activate(pair):
        frames = (2 * pair, 2 * pair + 1)
        means = group_means([frame_sum(s, None) for s in frames], gmat[...])
        variances = group_means([frame_sum(s, m) for s, m in zip(frames, means)], gmat[...])
        for s, m, var in zip(frames, means, variances):
            scale = lax.rsqrt(var + 1e-06)
            gain = gain1[...]
            empty = (c == 0) & (z < 4) & (q == 0) & (s < 2)

            def step(i, carry):
                v = (lat[s, i].astype(F32) - m) * scale * gain
                v = v / (1.0 + jnp.exp(-v))
                v = jnp.where(empty, 0.0, v)
                at = pl.ds(pl.multiple_of(32 * i + 32, 32), 32)
                act[s, at, 0:C] = jnp.where(col == 0, 0.0, pltpu.roll(v, 1, 0)).astype(BF)
                act[s, at, C : 2 * C] = v.astype(BF)
                act[s, at, 2 * C : 3 * C] = jnp.where(col == 31, 0.0, pltpu.roll(v, 31, 0)).astype(BF)
                return carry

            lax.fori_loop(0, 8, step, 0)

    activate(1)
    x3_stage(4)
    arrived(halo, lat_sem.at[0])
    activate(0)

    acc[...] = jnp.zeros_like(acc)

    def taps(ta):
        t, a = ta // 3, lax.rem(ta, 3)
        for j in range(2):
            rows = pl.ds(pl.multiple_of(32 * a, 32), 256)
            acc[j] += dot_nt(act[j + t, rows, :], wall[ta])

    def own_taps(i, carry):
        taps(near + i)
        return carry

    lax.fori_loop(0, 5, own_taps, 0)

    def sib_taps(n, carry):
        ta = jnp.where(c == 0, 5 + n, n)
        arrived(wall.at[ta], ssib.at[n])
        taps(ta)
        return carry

    lax.fori_loop(0, 4, sib_taps, 0)

    lane = iota((C, 128), 1)
    slot = lane >> 4
    chan = 12 * ((zc + 4 * (slot & 1)) * 4 + (slot >> 1)) + (lane & 15)
    pick = one_hot((iota((C, 128), 0) == chan) & ((lane & 15) < 12))
    for j in range(2):
        frame = lat[2 + j].reshape(256, C)
        thr_s[j] = (dot_nn(frame, pick) + acc[j]).astype(BF)

    for k in range(4):
        j = k % 2
        dst = thr.at[:, pl.ds(pl.multiple_of(128 * zc, 128), 128)]
        send_or_keep(thr_s.at[j], dst, exsem.at[zc], tm, 4 * g + k)
    q_stage(6)
    for k in range(4):
        arrived(thr.at[:, pl.ds(128 * k, 128)], exsem.at[k])

    part = iota((512, C), 0)
    slot = (part & 127) >> 4
    chan = 12 * (((part >> 7) + 4 * (slot & 1)) * 4 + (slot >> 1)) + (part & 15)
    pick_all = one_hot((iota((512, C), 1) == chan) & ((part & 15) < 12))
    through = dot_nn(thr[...], pick_all)
    thrn[...] = through

    mean = group_means([jnp.sum(through, axis=0, keepdims=True)], gmat[...])[0]
    dev = through - mean
    var = group_means([jnp.sum(dev * dev, axis=0, keepdims=True)], gmat[...])[0]
    normed = (dev * lax.rsqrt(var + 1e-06) * gain2[...]).astype(BF)
    thr[:, 0:C] = normed

    arrived(wq.at[pl.ds(2 * (1 - c), 2)], qsib)
    packed = iota((C, 512), 1)
    unpack = one_hot((iota((C, 512), 0) == 12 * (packed >> 4) + (packed & 15)) & ((packed & 15) < 12))
    w_value = dot_nn(unpack, wq[2]).astype(BF)
    w_out = dot_nn(unpack, wq[3]).astype(BF)
    mine_rows = pl.ds(pl.multiple_of(128 * half, 128), 128)
    queries = dot_nt(thr[mine_rows, 0:C], wq[0]).astype(BF)
    keys = dot_nt(normed, wq[1]).astype(BF)
    values = dot_nt(normed, w_value).astype(BF)
    scores = dot_nt(queries, keys) * (C ** -0.5)
    expon = jnp.exp(scores - jnp.max(scores, axis=1, keepdims=True))
    totals = jnp.sum(expon, axis=1, keepdims=True)
    attended = (dot_nn(expon.astype(BF), values) / totals).astype(BF)
    result = thrn[mine_rows, :] + dot_nt(attended, w_out)
    obuf[...] = result.astype(BF).reshape(4, 32, C)

    fr = 2 * c + fsel
    for k in range(4):
        send_or_keep(obuf.at[k], out_ref.at[fr], outsem.at[fr], 2 * q + g, 4 * half + k)
    for k in range(4):
        arrived(out_ref.at[k], outsem.at[k])

    for when, desc in pending:
        if when is None:
            desc.wait_send()
        else:
            pl.when(when)(desc.wait_send)


def body(latents, gain_one, conv_weight, gain_two, qkv_weight, out_weight):
    c = lax.rem(lax.axis_index("tm"), 2)
    taps = conv_weight.reshape(9, 3, C, 6).transpose(0, 3, 1, 2).reshape(9, 6, 3 * C)
    proj = jnp.concatenate([qkv_weight.transpose(0, 2, 1), out_weight.T[None]], 0)

    def placed(w):
        low = jnp.pad(w, ((0, 0), (0, 10), (0, 0)))
        high = jnp.pad(w, ((0, 0), (6, 4), (0, 0)))
        return jnp.where(c == 0, low, high)

    vmem = pl.BlockSpec(memory_space=pltpu.VMEM)
    dma = pltpu.SemaphoreType.DMA
    out = pl.pallas_call(
        kernel,
        out_shape=jax.ShapeDtypeStruct((4, 32, C), BF),
        in_specs=[pl.BlockSpec(memory_space=pl.ANY)] + [vmem] * 4,
        out_specs=vmem,
        scratch_shapes=[
            pltpu.VMEM((4, 8, 32, C), BF),
            pltpu.VMEM((5, 16, 3 * C), BF),
            pltpu.VMEM((2, 16, C), BF),
            pltpu.VMEM((9, 128, 3 * C), BF),
            pltpu.VMEM((4, 512, C), BF),
            pltpu.VMEM((4, 320, 3 * C), BF),
            pltpu.VMEM((2, 256, 128), F32),
            pltpu.VMEM((2, 256, 128), BF),
            pltpu.VMEM((256, 512), BF),
            pltpu.VMEM((256, C), F32),
            pltpu.VMEM((4, 32, C), BF),
            pltpu.VMEM((C, C), BF),
            dma((NSEND,)), dma((2,)), dma((2,)), dma((5,)), dma((5,)), dma((5,)), dma((5,)), dma((5,)), dma((5,)),
            dma((4,)), dma((4,)), dma((8,)), dma, dma((4,)), dma((4,)),
        ],
        compiler_params=pltpu.CompilerParams(
            collective_id=0, has_side_effects=True, vmem_limit_bytes=40 * 1024 * 1024
        ),
        cost_estimate=pl.CostEstimate(flops=2 * 10**9, bytes_accessed=10**7, transcendentals=10**6),
    )(latents[:, 0], placed(taps), placed(proj), gain_one[None], gain_two[None])
    return out[:, None]


def solution(mesh):
    in_specs = (
        P("tm", "rows", None, None),
        P(),
        P(None, None, "tm"),
        P(),
        P(None, None, "tm"),
        P(None, "tm"),
    )
    out_specs = P("tm", "rows", None, None)
    return jax.shard_map(body, mesh=mesh, in_specs=in_specs, out_specs=out_specs, check_vma=False)
```

```python
import jax
import jax.numpy as jnp
from jax import lax
from jax.experimental import pallas as pl
from jax.experimental.pallas import tpu as pltpu
from jax.sharding import PartitionSpec as P

C = 384
NX, NY, NZ = 4, 8, 8
BF = jnp.bfloat16
F32 = jnp.float32
MESH = pl.DeviceIdType.MESH
NSEND = 96


def iota(shape, dim):
    return lax.broadcasted_iota(jnp.int32, shape, dim)


def twelfth(i):
    return (i * 43691) >> 19


def one_hot(mask):
    return jnp.where(mask, 1.0, 0.0).astype(BF)


def dot_nn(a, b):
    return lax.dot_general(a, b, (((1,), (0,)), ((), ())), preferred_element_type=F32)


def dot_nt(a, b):
    return lax.dot_general(a, b, (((1,), (1,)), ((), ())), preferred_element_type=F32)


def group_means(sums, gmat):
    rows = iota((16, C), 0)
    stack = jnp.zeros((16, C), F32)
    for n, s in enumerate(sums):
        high = s.astype(BF).astype(F32)
        rest = s - high
        mid = rest.astype(BF).astype(F32)
        for k, part in enumerate((high, mid, rest - mid)):
            stack = jnp.where(rows == 3 * n + k, part, stack)
    res = dot_nn(stack.astype(BF), gmat)
    out = []
    for n in range(len(sums)):
        total = res[3 * n : 3 * n + 1] + res[3 * n + 1 : 3 * n + 2] + res[3 * n + 2 : 3 * n + 3]
        out.append(total * (1.0 / (12 * 256)))
    return out


def kernel(
    lat_in, wc_in, wq_in, gain1, gain2, out_ref,
    lat, sibc, sibq, wall, wq, act, acc, thr_s, thr, thrn, obuf, gmat,
    sends, lat_sem, sibw_sem, yp, ym, xp, xm, xpp, xmm, ssib, qx, qy, qsib, exsem, outsem,
):
    tm = lax.axis_index("tm")
    z = lax.axis_index("rows")
    c = lax.rem(tm, 2)
    q = tm // 2
    x = lax.rem(q, NX)
    y = q // NX
    g = z // 4
    zc = lax.rem(z, 4)
    half = zc // 2
    fsel = lax.rem(zc, 2)

    pending = []

    def place(yy, xx, core):
        return (lax.rem(yy + NY, NY) * NX + lax.rem(xx + NX, NX)) * 2 + core

    def send(src, dst, rsem, to_tm, to_z, when=None):
        d = pltpu.make_async_remote_copy(
            src_ref=src, dst_ref=dst, send_sem=sends.at[len(pending)], recv_sem=rsem,
            device_id=(to_tm, to_z), device_id_type=MESH,
        )
        if when is None:
            d.start()
        else:
            pl.when(when)(d.start)
        pending.append((when, d))

    def send_or_keep(src, dst, rsem, to_tm, to_z):
        here = jnp.logical_and(to_tm == tm, to_z == z)
        send(src, dst, rsem, to_tm, to_z, jnp.logical_not(here))
        pl.when(here)(pltpu.make_async_copy(src, dst, rsem).start)

    def arrived(ref, sem):
        pltpu.make_async_copy(ref, ref, sem).wait()

    barrier = pltpu.get_barrier_semaphore()

    def sends_to(c0, z0, c1, z1):
        a = z1 // 4 == c0
        a = a | ((c0 == 0) & (c1 == 0) & (z1 // 4 == 1))
        a = a | (z1 == z0)
        a = a | ((c1 == c0) & (z1 // 4 == z0 // 4))
        a = a | ((c1 == z0 // 4) & (z1 // 4 == lax.rem(z0, 4) // 2))
        return a & jnp.logical_not((c0 == c1) & (z0 == z1))

    def greet(i, count):
        co, zo = i // NZ, lax.rem(i, NZ)

        @pl.when(sends_to(co, zo, c, z))
        def _():
            pl.semaphore_signal(barrier, inc=1, device_id=(2 * q + co, zo), device_id_type=MESH)

        return count + jnp.where(sends_to(c, z, co, zo), 1, 0)

    count = lax.fori_loop(0, 2 * NZ, greet, jnp.int32(0))
    right, left = place(y, x + 1, c), place(y, x - 1, c)
    up, down = place(y + 1, x, c), place(y - 1, x, c)
    for other in (right, left, up, down):
        pl.semaphore_signal(barrier, inc=1, device_id=(other, z), device_id_type=MESH)
    prev_q = lax.rem(q + 31, 32)

    @pl.when((c == 0) & (z < 4))
    def _():
        def halo_greet(r, carry):
            pl.semaphore_signal(barrier, inc=1, device_id=(2 * prev_q + 1, r), device_id_type=MESH)
            return carry

        lax.fori_loop(0, NZ, halo_greet, 0)

    pl.semaphore_wait(barrier, count + 4 + 4 * c)

    sib = 2 * q + 1 - c
    d = lax.rem(y + 4 - zc, 4)
    source = d == 0

    near, far = 4 * c, 4 * (1 - c)
    send(wc_in.at[pl.ds(far, 5)], sibc, sibw_sem.at[0], sib, z, source)
    send(wq_in.at[pl.ds(2 * (1 - c), 2)], sibq, sibw_sem.at[1], sib, z)

    q_halo = lax.rem(q + c, 32)
    for k in range(4):
        send_or_keep(lat_in.at[pl.ds(0, 2)], lat.at[pl.ds(2, 2), z], lat_sem.at[1], 2 * q, 4 * c + k)
        send_or_keep(lat_in.at[pl.ds(2, 2)], lat.at[pl.ds(2, 2), z], lat_sem.at[1], 2 * q + 1, 4 * c + k)
        send_or_keep(lat_in.at[pl.ds(2, 2)], lat.at[pl.ds(0, 2), z], lat_sem.at[0], 2 * q_halo, 4 * (1 - c) + k)

    def rows_of(slot, n=1):
        return pl.ds(pl.multiple_of(16 * slot, 16), 16 * n)

    @pl.when(source)
    def _():
        arrived(sibc, sibw_sem.at[0])
        own = 2 * x + y // 4

        def merge(i, carry):
            wall[near + i, rows_of(own), :] = wc_in[near + i] + sibc[i]
            return carry

        lax.fori_loop(0, 5, merge, 0)

    arrived(sibq, sibw_sem.at[1])
    kinds = pl.ds(2 * c, 2)
    for k in range(2):
        wq[2 * c + k, rows_of(q), :] = wq_in[2 * c + k] + sibq[k]

    slot_right = 2 * x + lax.rem(y + 8 - d, 8) // 4
    slot_left = 2 * x + lax.rem(y + 8 + 4 - d, 8) // 4
    slot_left = jnp.where(source, 2 * x + y // 4, slot_left)
    slot_far = 2 * x + 1 - y // 4
    slot_in_p = jnp.where(source, slot_far, slot_right)
    slot_in_m = slot_left

    def wpart(i, slot, n=1):
        return wall.at[near + i, rows_of(slot, n), :]

    def post(src, rsem, to_tm, index):
        return pltpu.make_async_remote_copy(
            src_ref=src, dst_ref=src, send_sem=sends.at[index], recv_sem=rsem,
            device_id=(to_tm, z), device_id_type=MESH,
        )

    first_y = len(pending)
    ups = [post(wpart(i, slot_right), yp.at[i], up, first_y + i) for i in range(5)]
    downs = [post(wpart(i, slot_left), ym.at[i], down, first_y + 5 + i) for i in range(5)]
    pending.extend((None, d_up) for d_up in ups)
    pending.extend((d != 1, d_down) for d_down in downs)

    def go_up(i):
        arrived(wpart(i, slot_in_p), yp.at[i])
        ups[i].start()

    def go_down(i):
        arrived(wpart(i, slot_in_m), ym.at[i])
        downs[i].start()

    @pl.when(source)
    def _():
        for i in range(5):
            ups[i].start()
            downs[i].start()

    @pl.when(d == 1)
    def _():
        for i in range(5):
            go_up(i)
        for i in range(5):
            arrived(wpart(i, slot_in_m), ym.at[i])

    @pl.when(d == 2)
    def _():
        for i in range(5):
            go_up(i)
            go_down(i)

    @pl.when(d == 3)
    def _():
        for i in range(5):
            go_down(i)
        for i in range(5):
            go_up(i)

    xl, xr, xo = lax.rem(x + 3, 4), lax.rem(x + 1, 4), lax.rem(x + 2, 4)

    def x1_stage(i):
        @pl.when(source)
        def _():
            arrived(wpart(i, slot_in_p), yp.at[i])

        send(wpart(i, 2 * x, 2), wpart(i, 2 * x, 2), xp.at[i], right, z)
        send(wpart(i, 2 * x, 2), wpart(i, 2 * x, 2), xm.at[i], left, z)

    def x2_stage(i):
        arrived(wpart(i, 2 * xl, 2), xp.at[i])
        send(wpart(i, 2 * xl), wpart(i, 2 * xl), xpp.at[i], right, z)
        arrived(wpart(i, 2 * xr, 2), xm.at[i])
        send(wpart(i, 2 * xr + 1), wpart(i, 2 * xr + 1), xmm.at[i], left, z)

    def x3_stage(i):
        arrived(wpart(i, 2 * xo), xpp.at[i])
        arrived(wpart(i, 2 * xo + 1), xmm.at[i])
        n = jnp.where(c == 0, i, i - 1)
        whole = wall.at[near + i]
        when = None if 0 < i < 4 else (c == 0 if i == 0 else c == 1)
        n = jnp.clip(n, 0, 3)
        send(whole, whole, ssib.at[n], sib, z, when)

    def qpart(k, nk, slot, n):
        return wq.at[pl.ds(2 * c + k, nk), rows_of(slot, n), :]

    row = 4 * y

    def q_stage(s):
        if s == 0:
            own = qpart(0, 2, q, 1)
            send(own, own, qx.at[0], right, z)
            send(own, own, qx.at[1], left, z)
        elif s == 1:
            arrived(qpart(0, 2, row + xl, 1), qx.at[0])
            part = qpart(0, 1, row + xl, 1)
            send(part, part, qx.at[2], right, z)
            arrived(qpart(0, 2, row + xr, 1), qx.at[1])
            part = qpart(1, 1, row + xr, 1)
            send(part, part, qx.at[3], left, z)
        elif s == 2:
            arrived(qpart(0, 1, row + xo, 1), qx.at[2])
            arrived(qpart(1, 1, row + xo, 1), qx.at[3])
            block = qpart(0, 2, row, 4)
            send(block, block, qy.at[0], up, z)
            send(block, block, qy.at[1], down, z)
        elif s < 6:
            step = s - 2
            from_p = 4 * lax.rem(y + 8 - step, 8)
            from_m = 4 * lax.rem(y + step, 8)
            arrived(qpart(0, 2, from_p, 4), qy.at[2 * step - 2])
            part = qpart(0, 2, from_p, 4) if step < 3 else qpart(0, 1, from_p, 4)
            send(part, part, qy.at[2 * step], up, z)
            arrived(qpart(0, 2, from_m, 4), qy.at[2 * step - 1])
            part = qpart(0, 2, from_m, 4) if step < 3 else qpart(1, 1, from_m, 4)
            send(part, part, qy.at[2 * step + 1], down, z)
        else:
            far_row = 4 * lax.rem(y + 4, 8)
            arrived(qpart(0, 1, far_row, 4), qy.at[6])
            arrived(qpart(1, 1, far_row, 4), qy.at[7])
            both = wq.at[kinds]
            send(both, both, qsib, sib, z)

    def constants():
        gmat[...] = one_hot(twelfth(iota((C, C), 0)) == twelfth(iota((C, C), 1)))
        zero = jnp.zeros((32, 3 * C), BF)
        for s in range(4):
            act[s, 0:32, :] = zero
            act[s, 288:320, :] = zero

    q_stage(0)
    constants()
    for i in range(5):
        x1_stage(i)
    q_stage(1)
    for i in range(5):
        x2_stage(i)
    q_stage(2)

    mine, halo = lat.at[pl.ds(2, 2)], lat.at[pl.ds(0, 2)]
    arrived(mine, lat_sem.at[1])
    send(mine, halo, lat_sem.at[0], sib, z, c == 0)

    q_stage(3)
    for i in range(4):
        x3_stage(i)
    q_stage(4)

    def frame_sum(s, mean):
        def step(i, total):
            v = lat[s, i].astype(F32)
            if mean is not None:
                v = v - mean
                v = v * v
            return total + v

        return jnp.sum(lax.fori_loop(0, 8, step, jnp.zeros((32, C), F32)), axis=0, keepdims=True)

    col = iota((32, C), 0)

    def activate(pair):
        frames = (2 * pair, 2 * pair + 1)
        means = group_means([frame_sum(s, None) for s in frames], gmat[...])
        variances = group_means([frame_sum(s, m) for s, m in zip(frames, means)], gmat[...])
        for s, m, var in zip(frames, means, variances):
            scale = lax.rsqrt(var + 1e-06)
            gain = gain1[...]
            empty = (c == 0) & (z < 4) & (q == 0) & (s < 2)

            def step(i, carry):
                v = (lat[s, i].astype(F32) - m) * scale * gain
                v = v / (1.0 + jnp.exp(-v))
                v = jnp.where(empty, 0.0, v)
                at = pl.ds(pl.multiple_of(32 * i + 32, 32), 32)
                act[s, at, 0:C] = jnp.where(col == 0, 0.0, pltpu.roll(v, 1, 0)).astype(BF)
                act[s, at, C : 2 * C] = v.astype(BF)
                act[s, at, 2 * C : 3 * C] = jnp.where(col == 31, 0.0, pltpu.roll(v, 31, 0)).astype(BF)
                return carry

            lax.fori_loop(0, 8, step, 0)

    activate(1)
    x3_stage(4)
    q_stage(5)
    arrived(halo, lat_sem.at[0])
    activate(0)

    acc[...] = jnp.zeros_like(acc)

    def taps(ta):
        t, a = ta // 3, lax.rem(ta, 3)
        for j in range(2):
            rows = pl.ds(pl.multiple_of(32 * a, 32), 256)
            acc[j] += dot_nt(act[j + t, rows, :], wall[ta])

    def own_taps(i, carry):
        taps(near + i)
        return carry

    lax.fori_loop(0, 5, own_taps, 0)

    def sib_taps(n, carry):
        ta = jnp.where(c == 0, 5 + n, n)
        arrived(wall.at[ta], ssib.at[n])
        taps(ta)
        return carry

    lax.fori_loop(0, 4, sib_taps, 0)

    lane = iota((C, 128), 1)
    slot = lane >> 4
    chan = 12 * ((zc + 4 * (slot & 1)) * 4 + (slot >> 1)) + (lane & 15)
    pick = one_hot((iota((C, 128), 0) == chan) & ((lane & 15) < 12))
    for j in range(2):
        frame = lat[2 + j].reshape(256, C)
        thr_s[j] = (dot_nn(frame, pick) + acc[j]).astype(BF)

    for k in range(4):
        j = k % 2
        dst = thr.at[:, pl.ds(pl.multiple_of(128 * zc, 128), 128)]
        send_or_keep(thr_s.at[j], dst, exsem.at[zc], tm, 4 * g + k)
    q_stage(6)
    for k in range(4):
        arrived(thr.at[:, pl.ds(128 * k, 128)], exsem.at[k])

    part = iota((512, C), 0)
    slot = (part & 127) >> 4
    chan = 12 * (((part >> 7) + 4 * (slot & 1)) * 4 + (slot >> 1)) + (part & 15)
    pick_all = one_hot((iota((512, C), 1) == chan) & ((part & 15) < 12))
    through = dot_nn(thr[...], pick_all)
    thrn[...] = through

    mean = group_means([jnp.sum(through, axis=0, keepdims=True)], gmat[...])[0]
    dev = through - mean
    var = group_means([jnp.sum(dev * dev, axis=0, keepdims=True)], gmat[...])[0]
    normed = (dev * lax.rsqrt(var + 1e-06) * gain2[...]).astype(BF)
    thr[:, 0:C] = normed

    arrived(wq.at[pl.ds(2 * (1 - c), 2)], qsib)
    packed = iota((C, 512), 1)
    unpack = one_hot((iota((C, 512), 0) == 12 * (packed >> 4) + (packed & 15)) & ((packed & 15) < 12))
    w_value = dot_nn(unpack, wq[2]).astype(BF)
    w_out = dot_nn(unpack, wq[3]).astype(BF)
    mine_rows = pl.ds(pl.multiple_of(128 * half, 128), 128)
    queries = dot_nt(thr[mine_rows, 0:C], wq[0]).astype(BF)
    keys = dot_nt(normed, wq[1]).astype(BF)
    values = dot_nt(normed, w_value).astype(BF)
    scores = dot_nt(queries, keys) * (C ** -0.5)
    expon = jnp.exp(scores - jnp.max(scores, axis=1, keepdims=True))
    totals = jnp.sum(expon, axis=1, keepdims=True)
    attended = (dot_nn(expon.astype(BF), values) / totals).astype(BF)
    result = thrn[mine_rows, :] + dot_nt(attended, w_out)
    obuf[...] = result.astype(BF).reshape(4, 32, C)

    fr = 2 * c + fsel
    for k in range(4):
        send_or_keep(obuf.at[k], out_ref.at[fr], outsem.at[fr], 2 * q + g, 4 * half + k)
    for k in range(4):
        arrived(out_ref.at[k], outsem.at[k])

    for when, desc in pending:
        if when is None:
            desc.wait_send()
        else:
            pl.when(when)(desc.wait_send)


def body(latents, gain_one, conv_weight, gain_two, qkv_weight, out_weight):
    c = lax.rem(lax.axis_index("tm"), 2)
    taps = conv_weight.reshape(9, 3, C, 6).transpose(0, 3, 1, 2).reshape(9, 6, 3 * C)
    proj = jnp.concatenate([qkv_weight.transpose(0, 2, 1), out_weight.T[None]], 0)

    def placed(w):
        low = jnp.pad(w, ((0, 0), (0, 10), (0, 0)))
        high = jnp.pad(w, ((0, 0), (6, 4), (0, 0)))
        return jnp.where(c == 0, low, high)

    vmem = pl.BlockSpec(memory_space=pltpu.VMEM)
    dma = pltpu.SemaphoreType.DMA
    out = pl.pallas_call(
        kernel,
        out_shape=jax.ShapeDtypeStruct((4, 32, C), BF),
        in_specs=[pl.BlockSpec(memory_space=pl.ANY)] + [vmem] * 4,
        out_specs=vmem,
        scratch_shapes=[
            pltpu.VMEM((4, 8, 32, C), BF),
            pltpu.VMEM((5, 16, 3 * C), BF),
            pltpu.VMEM((2, 16, C), BF),
            pltpu.VMEM((9, 128, 3 * C), BF),
            pltpu.VMEM((4, 512, C), BF),
            pltpu.VMEM((4, 320, 3 * C), BF),
            pltpu.VMEM((2, 256, 128), F32),
            pltpu.VMEM((2, 256, 128), BF),
            pltpu.VMEM((256, 512), BF),
            pltpu.VMEM((256, C), F32),
            pltpu.VMEM((4, 32, C), BF),
            pltpu.VMEM((C, C), BF),
            dma((NSEND,)), dma((2,)), dma((2,)), dma((5,)), dma((5,)), dma((5,)), dma((5,)), dma((5,)), dma((5,)),
            dma((4,)), dma((4,)), dma((8,)), dma, dma((4,)), dma((4,)),
        ],
        compiler_params=pltpu.CompilerParams(
            collective_id=0, has_side_effects=True, vmem_limit_bytes=40 * 1024 * 1024
        ),
        cost_estimate=pl.CostEstimate(flops=2 * 10**9, bytes_accessed=10**7, transcendentals=10**6),
    )(latents[:, 0], placed(taps), placed(proj), gain_one[None], gain_two[None])
    return out[:, None]


def solution(mesh):
    in_specs = (
        P("tm", "rows", None, None),
        P(),
        P(None, None, "tm"),
        P(),
        P(None, None, "tm"),
        P(None, "tm"),
    )
    out_specs = P("tm", "rows", None, None)
    return jax.shard_map(body, mesh=mesh, in_specs=in_specs, out_specs=out_specs, check_vma=False)
```

```python
import jax
import jax.numpy as jnp
from jax import lax
from jax.experimental import pallas as pl
from jax.experimental.pallas import tpu as pltpu
from jax.sharding import PartitionSpec as P

C = 384
NX, NY, NZ = 4, 8, 8
BF = jnp.bfloat16
F32 = jnp.float32
MESH = pl.DeviceIdType.MESH
NSEND = 96


def iota(shape, dim):
    return lax.broadcasted_iota(jnp.int32, shape, dim)


def twelfth(i):
    return (i * 43691) >> 19


def one_hot(mask):
    return jnp.where(mask, 1.0, 0.0).astype(BF)


def dot_nn(a, b):
    return lax.dot_general(a, b, (((1,), (0,)), ((), ())), preferred_element_type=F32)


def dot_nt(a, b):
    return lax.dot_general(a, b, (((1,), (1,)), ((), ())), preferred_element_type=F32)


def group_means(sums, gmat):
    rows = iota((16, C), 0)
    stack = jnp.zeros((16, C), F32)
    for n, s in enumerate(sums):
        high = s.astype(BF).astype(F32)
        rest = s - high
        mid = rest.astype(BF).astype(F32)
        for k, part in enumerate((high, mid, rest - mid)):
            stack = jnp.where(rows == 3 * n + k, part, stack)
    res = dot_nn(stack.astype(BF), gmat)
    out = []
    for n in range(len(sums)):
        total = res[3 * n : 3 * n + 1] + res[3 * n + 1 : 3 * n + 2] + res[3 * n + 2 : 3 * n + 3]
        out.append(total * (1.0 / (12 * 256)))
    return out


def kernel(
    lat_in, wc_in, wq_in, gain1_in, gain2_in, out_ref,
    lat, sibc, sibq, own, wall, wq, act, acc, thr_s, thr, thrn, obuf, gmat, pick, pick_all, unpack, gain1, gain2,
    sends, lat_sem, sibw_sem, yp, ym, xp, xm, xpp, xmm, ssib, qx, qy, qsib, exsem, outsem, gain_sem,
):
    tm = lax.axis_index("tm")
    z = lax.axis_index("rows")
    c = lax.rem(tm, 2)
    q = tm // 2
    x = lax.rem(q, NX)
    y = q // NX
    g = z // 4
    zc = lax.rem(z, 4)
    half = zc // 2
    fsel = lax.rem(zc, 2)

    pending = []

    def place(yy, xx, core):
        return (lax.rem(yy + NY, NY) * NX + lax.rem(xx + NX, NX)) * 2 + core

    def send(src, dst, rsem, to_tm, to_z, when=None):
        d = pltpu.make_async_remote_copy(
            src_ref=src, dst_ref=dst, send_sem=sends.at[len(pending)], recv_sem=rsem,
            device_id=(to_tm, to_z), device_id_type=MESH,
        )
        if when is None:
            d.start()
        else:
            pl.when(when)(d.start)
        pending.append((when, d))

    def send_or_keep(src, dst, rsem, to_tm, to_z):
        here = jnp.logical_and(to_tm == tm, to_z == z)
        send(src, dst, rsem, to_tm, to_z, jnp.logical_not(here))
        pl.when(here)(pltpu.make_async_copy(src, dst, rsem).start)

    def arrived(ref, sem):
        pltpu.make_async_copy(ref, ref, sem).wait()

    for k, (src, dst) in enumerate(((gain1_in, gain1), (gain2_in, gain2))):
        pltpu.make_async_copy(src, dst, gain_sem.at[k]).start()

    barrier = pltpu.get_barrier_semaphore()

    def sends_to(c0, z0, c1, z1):
        a = z1 // 4 == c0
        a = a | ((c0 == 0) & (c1 == 0) & (z1 // 4 == 1))
        a = a | (z1 == z0)
        a = a | ((c1 == c0) & (z1 // 4 == z0 // 4))
        a = a | ((c1 == z0 // 4) & (z1 // 4 == lax.rem(z0, 4) // 2))
        return a & jnp.logical_not((c0 == c1) & (z0 == z1))

    def greet(i, count):
        co, zo = i // NZ, lax.rem(i, NZ)

        @pl.when(sends_to(co, zo, c, z))
        def _():
            pl.semaphore_signal(barrier, inc=1, device_id=(2 * q + co, zo), device_id_type=MESH)

        return count + jnp.where(sends_to(c, z, co, zo), 1, 0)

    count = lax.fori_loop(0, 2 * NZ, greet, jnp.int32(0))
    right, left = place(y, x + 1, c), place(y, x - 1, c)
    near_y = [place(y + step, x, c) for step in (1, -1, 2, -2)]
    for other in [right, left] + near_y:
        pl.semaphore_signal(barrier, inc=1, device_id=(other, z), device_id_type=MESH)

    @pl.when(zc == 0)
    def _():
        pl.semaphore_signal(barrier, inc=1, device_id=(place(y + 4, x, c), z), device_id_type=MESH)

    @pl.when(zc == 3)
    def _():
        for step in (3, -3):
            pl.semaphore_signal(barrier, inc=1, device_id=(place(y + step, x, c), z), device_id_type=MESH)

    prev_q = lax.rem(q + 31, 32)

    @pl.when((c == 0) & (z < 4))
    def _():
        def halo_greet(r, carry):
            pl.semaphore_signal(barrier, inc=1, device_id=(2 * prev_q + 1, r), device_id_type=MESH)
            return carry

        lax.fori_loop(0, NZ, halo_greet, 0)

    pl.semaphore_wait(barrier, count + 6 + 4 * c + jnp.where(zc == 0, 1, 0) + jnp.where(zc == 3, 2, 0))

    sib = 2 * q + 1 - c
    far_row = jnp.where(zc == 0, 4, -zc)

    near, far = 4 * c, 4 * (1 - c)
    send(wc_in.at[pl.ds(far, 5)], sibc, sibw_sem.at[0], sib, z)
    send(wq_in.at[pl.ds(2 * (1 - c), 2)], sibq, sibw_sem.at[1], sib, z)

    q_halo = lax.rem(q + c, 32)
    for k in range(4):
        send_or_keep(lat_in.at[pl.ds(0, 2)], lat.at[pl.ds(2, 2), z], lat_sem.at[1], 2 * q, 4 * c + k)
        send_or_keep(lat_in.at[pl.ds(2, 2)], lat.at[pl.ds(2, 2), z], lat_sem.at[1], 2 * q + 1, 4 * c + k)
        send_or_keep(lat_in.at[pl.ds(2, 2)], lat.at[pl.ds(0, 2), z], lat_sem.at[0], 2 * q_halo, 4 * (1 - c) + k)

    def rows_of(slot, n=1):
        return pl.ds(pl.multiple_of(16 * slot, 16), 16 * n)

    kinds = pl.ds(2 * c, 2)

    def wpart(i, slot, n=1):
        return wall.at[near + i, rows_of(slot, n), :]

    def post(src, rsem, to_tm, index):
        return pltpu.make_async_remote_copy(
            src_ref=src, dst_ref=src, send_sem=sends.at[index], recv_sem=rsem,
            device_id=(to_tm, z), device_id_type=MESH,
        )

    to_first, to_second = place(y - zc, x, c), place(y - far_row, x, c)
    arrived(sibc, sibw_sem.at[0])
    for i in range(5):
        own[i] = wc_in[near + i] + sibc[i]
        for h, (to, sem) in enumerate(((to_first, yp), (to_second, ym))):
            copy = pltpu.make_async_remote_copy(
                src_ref=own.at[i], dst_ref=wpart(i, 2 * x + h), send_sem=sends.at[len(pending)],
                recv_sem=sem.at[i], device_id=(to, z), device_id_type=MESH,
            )
            when = zc != 0 if h == 0 else None
            if h == 0:
                pl.when(zc != 0)(copy.start)
            else:
                copy.start()
            pending.append((when, copy))

    arrived(sibq, sibw_sem.at[1])
    for k in range(2):
        wq[2 * c + k, rows_of(q), :] = wq_in[2 * c + k] + sibq[k]

    xl, xr, xo = lax.rem(x + 3, 4), lax.rem(x + 1, 4), lax.rem(x + 2, 4)

    first_x = len(pending)
    rights = [post(wpart(i, 2 * x, 2), xp.at[i], right, first_x + i) for i in range(5)]
    lefts = [post(wpart(i, 2 * x, 2), xm.at[i], left, first_x + 5 + i) for i in range(5)]
    pending.extend((None, copy) for copy in rights + lefts)

    def x1_stage(i):
        @pl.when(zc == 0)
        def _():
            wall[near + i, rows_of(2 * x), :] = own[i]

        @pl.when(zc != 0)
        def _():
            arrived(wpart(i, 2 * x), yp.at[i])

        arrived(wpart(i, 2 * x + 1), ym.at[i])
        rights[i].start()
        lefts[i].start()

    def x2_stage(i):
        arrived(wpart(i, 2 * xl, 2), xp.at[i])
        send(wpart(i, 2 * xl), wpart(i, 2 * xl), xpp.at[i], right, z)
        arrived(wpart(i, 2 * xr, 2), xm.at[i])
        send(wpart(i, 2 * xr + 1), wpart(i, 2 * xr + 1), xmm.at[i], left, z)

    def x3_stage(i):
        arrived(wpart(i, 2 * xo), xpp.at[i])
        arrived(wpart(i, 2 * xo + 1), xmm.at[i])
        n = jnp.where(c == 0, i, i - 1)
        whole = wall.at[near + i]
        when = None if 0 < i < 4 else (c == 0 if i == 0 else c == 1)
        n = jnp.clip(n, 0, 3)
        send(whole, whole, ssib.at[n], sib, z, when)

    def qpart(k, nk, slot, n):
        return wq.at[pl.ds(2 * c + k, nk), rows_of(slot, n), :]

    row = 4 * y

    def q_row(step):
        return 4 * lax.rem(y + 8 + step, 8)

    def q_stage(s):
        if s == 0:
            own = qpart(0, 2, q, 1)
            send(own, own, qx.at[0], right, z)
            send(own, own, qx.at[1], left, z)
        elif s == 1:
            arrived(qpart(0, 2, row + xl, 1), qx.at[0])
            part = qpart(0, 1, row + xl, 1)
            send(part, part, qx.at[2], right, z)
            arrived(qpart(0, 2, row + xr, 1), qx.at[1])
            part = qpart(1, 1, row + xr, 1)
            send(part, part, qx.at[3], left, z)
        elif s == 2:
            arrived(qpart(0, 1, row + xo, 1), qx.at[2])
            arrived(qpart(1, 1, row + xo, 1), qx.at[3])
            block = qpart(0, 2, row, 4)
            for n in range(4):
                send(block, block, qy.at[n], near_y[n], z)
        elif s == 3:
            for n, step in enumerate((-1, 1, -2, 2)):
                arrived(qpart(0, 2, q_row(step), 4), qy.at[n])
            for n, (step, k, nk) in enumerate(((-1, 0, 2), (1, 0, 2), (-2, 0, 1), (2, 1, 1))):
                block = qpart(k, nk, q_row(step), 4)
                send(block, block, qy.at[4 + n], near_y[2 + n % 2], z)
        else:
            for n, (step, k, nk) in enumerate(((-3, 0, 2), (3, 0, 2), (4, 0, 1), (4, 1, 1))):
                arrived(qpart(k, nk, q_row(step), 4), qy.at[4 + n])
            both = wq.at[kinds]
            send(both, both, qsib, sib, z)

    def constants():
        gmat[...] = one_hot(twelfth(iota((C, C), 0)) == twelfth(iota((C, C), 1)))
        zero = jnp.zeros((32, 3 * C), BF)
        for s in range(4):
            act[s, 0:32, :] = zero
            act[s, 288:320, :] = zero
        def channel(place_in, k):
            slot = (place_in & 127) >> 4
            row_of = (y + 8 + jnp.where((slot & 1) == 0, k, jnp.where(k == 0, 4, -k))) & 7
            return 12 * (row_of * 4 + (slot >> 1)) + (place_in & 15)

        lane = iota((C, 128), 1)
        chan = channel(lane, zc)
        pick[...] = one_hot((iota((C, 128), 0) == chan) & ((lane & 15) < 12))
        part = iota((512, C), 0)
        chan = channel(part, part >> 7)
        pick_all[...] = one_hot((iota((512, C), 1) == chan) & ((part & 15) < 12))
        packed = iota((C, 512), 1)
        unpack[...] = one_hot((iota((C, 512), 0) == 12 * (packed >> 4) + (packed & 15)) & ((packed & 15) < 12))

    mine, halo = lat.at[pl.ds(2, 2)], lat.at[pl.ds(0, 2)]

    def frame_sum(s, mean):
        def step(i, total):
            v = lat[s, i].astype(F32)
            if mean is not None:
                v = v - mean
                v = v * v
            return total + v

        return jnp.sum(lax.fori_loop(0, 8, step, jnp.zeros((32, C), F32)), axis=0, keepdims=True)

    col = iota((32, C), 0)

    def activate(pair):
        frames = (2 * pair, 2 * pair + 1)
        means = group_means([frame_sum(s, None) for s in frames], gmat[...])
        variances = group_means([frame_sum(s, m) for s, m in zip(frames, means)], gmat[...])
        for s, m, var in zip(frames, means, variances):
            scale = lax.rsqrt(var + 1e-06)
            gain = gain1[...].reshape(1, C)
            empty = (c == 0) & (z < 4) & (q == 0) & (s < 2)

            def step(i, carry):
                v = (lat[s, i].astype(F32) - m) * scale * gain
                v = v / (1.0 + jnp.exp(-v))
                v = jnp.where(empty, 0.0, v)
                at = pl.ds(pl.multiple_of(32 * i + 32, 32), 32)
                act[s, at, 0:C] = jnp.where(col == 0, 0.0, pltpu.roll(v, 1, 0)).astype(BF)
                act[s, at, C : 2 * C] = v.astype(BF)
                act[s, at, 2 * C : 3 * C] = jnp.where(col == 31, 0.0, pltpu.roll(v, 31, 0)).astype(BF)
                return carry

            lax.fori_loop(0, 8, step, 0)

    def taps(ta):
        t, a = ta // 3, lax.rem(ta, 3)
        for j in range(2):
            rows = pl.ds(pl.multiple_of(32 * a, 32), 256)
            acc[j] += dot_nt(act[j + t, rows, :], wall[ta])

    def own_taps(i):
        x3_stage(i)
        taps(near + i)

    q_stage(0)
    constants()
    arrived(gain1, gain_sem.at[0])
    arrived(gain2, gain_sem.at[1])
    x1_stage(0)
    x1_stage(1)
    q_stage(1)
    x1_stage(2)
    x2_stage(0)
    x1_stage(3)
    x2_stage(1)
    q_stage(2)
    x1_stage(4)
    x2_stage(2)
    arrived(mine, lat_sem.at[1])
    send(mine, halo, lat_sem.at[0], sib, z, c == 0)
    for j in range(2):
        acc[j] = dot_nn(lat[2 + j].reshape(256, C), pick[...])
    activate(1)
    x2_stage(3)
    q_stage(3)
    arrived(halo, lat_sem.at[0])
    activate(0)
    x2_stage(4)
    own_taps(0)
    own_taps(1)
    q_stage(4)
    own_taps(2)
    own_taps(3)
    own_taps(4)

    def sib_taps(n, carry):
        ta = jnp.where(c == 0, 5 + n, n)
        arrived(wall.at[ta], ssib.at[n])
        taps(ta)
        return carry

    lax.fori_loop(0, 4, sib_taps, 0)
    for j in range(2):
        thr_s[j] = acc[j].astype(BF)

    for k in range(4):
        j = k % 2
        dst = thr.at[:, pl.ds(pl.multiple_of(128 * zc, 128), 128)]
        send_or_keep(thr_s.at[j], dst, exsem.at[zc], tm, 4 * g + k)
    arrived(wq.at[pl.ds(2 * (1 - c), 2)], qsib)
    w_value = dot_nn(unpack[...], wq[2]).astype(BF)
    w_out = dot_nn(unpack[...], wq[3]).astype(BF)
    for k in range(4):
        arrived(thr.at[:, pl.ds(128 * k, 128)], exsem.at[k])

    through = dot_nn(thr[...], pick_all[...])
    thrn[...] = through

    mean = group_means([jnp.sum(through, axis=0, keepdims=True)], gmat[...])[0]
    dev = through - mean
    var = group_means([jnp.sum(dev * dev, axis=0, keepdims=True)], gmat[...])[0]
    normed = (dev * lax.rsqrt(var + 1e-06) * gain2[...].reshape(1, C)).astype(BF)
    thr[:, 0:C] = normed

    mine_rows = pl.ds(pl.multiple_of(128 * half, 128), 128)
    queries = dot_nt(thr[mine_rows, 0:C], wq[0]).astype(BF)
    keys = dot_nt(normed, wq[1]).astype(BF)
    values = dot_nt(normed, w_value).astype(BF)
    scores = dot_nt(queries, keys) * (C ** -0.5)
    expon = jnp.exp(scores - jnp.max(scores, axis=1, keepdims=True))
    totals = jnp.sum(expon, axis=1, keepdims=True)
    attended = (dot_nn(expon.astype(BF), values) / totals).astype(BF)
    result = thrn[mine_rows, :] + dot_nt(attended, w_out)
    obuf[...] = result.astype(BF).reshape(4, 32, C)

    fr = 2 * c + fsel
    for k in range(4):
        send_or_keep(obuf.at[k], out_ref.at[fr], outsem.at[fr], 2 * q + g, 4 * half + k)
    for k in range(4):
        arrived(out_ref.at[k], outsem.at[k])

    for when, desc in pending:
        if when is None:
            desc.wait_send()
        else:
            pl.when(when)(desc.wait_send)


def body(latents, gain_one, conv_weight, gain_two, qkv_weight, out_weight):
    c = lax.rem(lax.axis_index("tm"), 2)
    taps = conv_weight.reshape(9, 3, C, 6).transpose(0, 3, 1, 2).reshape(9, 6, 3 * C)
    proj = jnp.concatenate([qkv_weight.transpose(0, 2, 1), out_weight.T[None]], 0)

    def placed(w):
        low = jnp.pad(w, ((0, 0), (0, 10), (0, 0)))
        high = jnp.pad(w, ((0, 0), (6, 4), (0, 0)))
        return jnp.where(c == 0, low, high)

    vmem = pl.BlockSpec(memory_space=pltpu.VMEM)
    anywhere = pl.BlockSpec(memory_space=pl.ANY)
    dma = pltpu.SemaphoreType.DMA
    out = pl.pallas_call(
        kernel,
        out_shape=jax.ShapeDtypeStruct((4, 32, C), BF),
        in_specs=[anywhere, vmem, vmem, anywhere, anywhere],
        out_specs=vmem,
        scratch_shapes=[
            pltpu.VMEM((4, 8, 32, C), BF),
            pltpu.VMEM((5, 16, 3 * C), BF),
            pltpu.VMEM((2, 16, C), BF),
            pltpu.VMEM((5, 16, 3 * C), BF),
            pltpu.VMEM((9, 128, 3 * C), BF),
            pltpu.VMEM((4, 512, C), BF),
            pltpu.VMEM((4, 320, 3 * C), BF),
            pltpu.VMEM((2, 256, 128), F32),
            pltpu.VMEM((2, 256, 128), BF),
            pltpu.VMEM((256, 512), BF),
            pltpu.VMEM((256, C), F32),
            pltpu.VMEM((4, 32, C), BF),
            pltpu.VMEM((C, C), BF),
            pltpu.VMEM((C, 128), BF),
            pltpu.VMEM((512, C), BF),
            pltpu.VMEM((C, 512), BF),
            pltpu.VMEM((C,), F32),
            pltpu.VMEM((C,), F32),
            dma((NSEND,)), dma((2,)), dma((2,)), dma((5,)), dma((5,)), dma((5,)), dma((5,)), dma((5,)), dma((5,)),
            dma((4,)), dma((4,)), dma((8,)), dma, dma((4,)), dma((4,)), dma((2,)),
        ],
        compiler_params=pltpu.CompilerParams(
            collective_id=0, has_side_effects=True, vmem_limit_bytes=40 * 1024 * 1024
        ),
        cost_estimate=pl.CostEstimate(flops=2 * 10**9, bytes_accessed=10**7, transcendentals=10**6),
    )(latents[:, 0], placed(taps), placed(proj), gain_one, gain_two)
    return out[:, None]


def solution(mesh):
    in_specs = (
        P("tm", "rows", None, None),
        P(),
        P(None, None, "tm"),
        P(),
        P(None, None, "tm"),
        P(None, "tm"),
    )
    out_specs = P("tm", "rows", None, None)
    return jax.shard_map(body, mesh=mesh, in_specs=in_specs, out_specs=out_specs, check_vma=False)
```

```python
import jax
import jax.numpy as jnp
from jax import lax
from jax.experimental import pallas as pl
from jax.experimental.pallas import tpu as pltpu
from jax.sharding import PartitionSpec as P

C = 384
NX, NY, NZ = 4, 8, 8
BF = jnp.bfloat16
F32 = jnp.float32
MESH = pl.DeviceIdType.MESH
NSEND = 96


def iota(shape, dim):
    return lax.broadcasted_iota(jnp.int32, shape, dim)


def twelfth(i):
    return (i * 43691) >> 19


def one_hot(mask):
    return jnp.where(mask, 1.0, 0.0).astype(BF)


def dot_nn(a, b):
    return lax.dot_general(a, b, (((1,), (0,)), ((), ())), preferred_element_type=F32)


def dot_nt(a, b):
    return lax.dot_general(a, b, (((1,), (1,)), ((), ())), preferred_element_type=F32)


def group_means(sums, gmat):
    rows = iota((16, C), 0)
    stack = jnp.zeros((16, C), F32)
    for n, s in enumerate(sums):
        high = s.astype(BF).astype(F32)
        rest = s - high
        mid = rest.astype(BF).astype(F32)
        for k, part in enumerate((high, mid, rest - mid)):
            stack = jnp.where(rows == 3 * n + k, part, stack)
    res = dot_nn(stack.astype(BF), gmat)
    out = []
    for n in range(len(sums)):
        total = res[3 * n : 3 * n + 1] + res[3 * n + 1 : 3 * n + 2] + res[3 * n + 2 : 3 * n + 3]
        out.append(total * (1.0 / (12 * 256)))
    return out


def kernel(
    lat_in, wc_in, wq_in, gain1_in, gain2_in, out_ref,
    lat, wc, sibc, sibq, own, mid, wall, wq, act, acc, thr_s, thr, thrn, obuf, gmat, pick, pick_all, unpack, widen, gain1, gain2,
    sends, lat_sem, sibw_sem, yp, ym, xp, xm, xpp, xmm, ssib, qx, qy, qsib, exsem, outsem, gain_sem, mid_sem,
):
    tm = lax.axis_index("tm")
    z = lax.axis_index("rows")
    c = lax.rem(tm, 2)
    q = tm // 2
    x = lax.rem(q, NX)
    y = q // NX
    g = z // 4
    zc = lax.rem(z, 4)
    half = zc // 2
    fsel = lax.rem(zc, 2)

    pending = []

    def place(yy, xx, core):
        return (lax.rem(yy + NY, NY) * NX + lax.rem(xx + NX, NX)) * 2 + core

    def send(src, dst, rsem, to_tm, to_z, when=None):
        d = pltpu.make_async_remote_copy(
            src_ref=src, dst_ref=dst, send_sem=sends.at[len(pending)], recv_sem=rsem,
            device_id=(to_tm, to_z), device_id_type=MESH,
        )
        if when is None:
            d.start()
        else:
            pl.when(when)(d.start)
        pending.append((when, d))

    def send_or_keep(src, dst, rsem, to_tm, to_z):
        here = jnp.logical_and(to_tm == tm, to_z == z)
        send(src, dst, rsem, to_tm, to_z, jnp.logical_not(here))
        pl.when(here)(pltpu.make_async_copy(src, dst, rsem).start)

    def arrived(ref, sem):
        pltpu.make_async_copy(ref, ref, sem).wait()

    for k, (src, dst) in enumerate(((gain1_in, gain1), (gain2_in, gain2))):
        pltpu.make_async_copy(src, dst, gain_sem.at[k]).start()

    barrier = pltpu.get_barrier_semaphore()

    def sends_to(c0, z0, c1, z1):
        a = z1 // 4 == c0
        a = a | ((c0 == 0) & (c1 == 0) & (z1 // 4 == 1))
        a = a | (z1 == z0)
        a = a | ((c1 == c0) & (z1 // 4 == z0 // 4))
        a = a | ((c1 == z0 // 4) & (z1 // 4 == lax.rem(z0, 4) // 2))
        return a & jnp.logical_not((c0 == c1) & (z0 == z1))

    def greet(i, count):
        co, zo = i // NZ, lax.rem(i, NZ)

        @pl.when(sends_to(co, zo, c, z))
        def _():
            pl.semaphore_signal(barrier, inc=1, device_id=(2 * q + co, zo), device_id_type=MESH)

        return count + jnp.where(sends_to(c, z, co, zo), 1, 0)

    count = lax.fori_loop(0, 2 * NZ, greet, jnp.int32(0))
    right, left = place(y, x + 1, c), place(y, x - 1, c)
    near_y = [place(y + step, x, c) for step in (1, -1, 2, -2)]
    for other in [right, left] + near_y:
        pl.semaphore_signal(barrier, inc=1, device_id=(other, z), device_id_type=MESH)

    @pl.when(zc == 3)
    def _():
        for step in (3, -3):
            pl.semaphore_signal(barrier, inc=1, device_id=(place(y + step, x, c), z), device_id_type=MESH)

    prev_q = lax.rem(q + 31, 32)

    @pl.when((c == 0) & (z < 4))
    def _():
        def halo_greet(r, carry):
            pl.semaphore_signal(barrier, inc=1, device_id=(2 * prev_q + 1, r), device_id_type=MESH)
            return carry

        lax.fori_loop(0, NZ, halo_greet, 0)

    raw = wc_in[...].reshape(192, C)
    r16, unit = iota((112, 192), 0) & 15, iota((112, 192), 0) >> 4
    third = twelfth(4 * unit)
    tail = r16 >= 12
    chan_of = jnp.where(tail, 4 * (unit - 3 * third) + r16 - 12, r16)
    tap_row = jnp.where(tail, 7 + third, unit)
    shard_row, tap = iota((112, 192), 1) >> 5, iota((112, 192), 1) & 31
    for b in range(3):
        wanted = (chan_of == 6 * c + shard_row) & (tap == 3 * tap_row + b) & (tap_row < 9)
        wc[:, :, b * C : (b + 1) * C] = dot_nn(one_hot(wanted), raw).astype(BF).reshape(7, 16, C)

    pl.semaphore_wait(barrier, count + 6 + 4 * c + jnp.where(zc == 3, 2, 0))

    sib = 2 * q + 1 - c
    far_row = jnp.where(zc == 0, 4, -zc)

    near, far = 3 * c, 3 * (1 - c)
    send(wc.at[pl.ds(far, 4)], sibc, sibw_sem.at[0], sib, z)
    send(wq_in.at[pl.ds(2 * (1 - c), 2)], sibq, sibw_sem.at[1], sib, z)

    q_halo = lax.rem(q + c, 32)
    for k in range(4):
        send_or_keep(lat_in.at[pl.ds(0, 2)], lat.at[pl.ds(2, 2), z], lat_sem.at[1], 2 * q, 4 * c + k)
        send_or_keep(lat_in.at[pl.ds(2, 2)], lat.at[pl.ds(2, 2), z], lat_sem.at[1], 2 * q + 1, 4 * c + k)
        send_or_keep(lat_in.at[pl.ds(2, 2)], lat.at[pl.ds(0, 2), z], lat_sem.at[0], 2 * q_halo, 4 * (1 - c) + k)

    def rows_of(slot, n=1):
        return pl.ds(pl.multiple_of(16 * slot, 16), 16 * n)

    kinds = pl.ds(2 * c, 2)

    def wpart(i, slot, n=1):
        return wall.at[near + i, rows_of(slot, n), :]

    def post(src, rsem, to_tm, index):
        return pltpu.make_async_remote_copy(
            src_ref=src, dst_ref=src, send_sem=sends.at[index], recv_sem=rsem,
            device_id=(to_tm, z), device_id_type=MESH,
        )

    to_first, to_second = place(y - zc, x, c), place(y - far_row, x, c)
    arrived(sibc, sibw_sem.at[0])
    for i in range(4):
        own[i] = wc[near + i] + sibc[i]
        for h, (to, sem) in enumerate(((to_first, yp), (to_second, ym))):
            copy = pltpu.make_async_remote_copy(
                src_ref=own.at[i], dst_ref=wpart(i, 2 * x + h), send_sem=sends.at[len(pending)],
                recv_sem=sem.at[i], device_id=(to, z), device_id_type=MESH,
            )
            pl.when(zc != 0)(copy.start)
            pending.append((zc != 0, copy))

    hops = []
    for i in range(4):
        for src, dst, sem in ((own.at[i], mid.at[i], mid_sem), (mid.at[i], wpart(i, 2 * x + 1), ym)):
            copy = pltpu.make_async_remote_copy(
                src_ref=src, dst_ref=dst, send_sem=sends.at[len(pending)], recv_sem=sem.at[i],
                device_id=(near_y[2 + i % 2], z), device_id_type=MESH,
            )
            pending.append((zc == 0, copy))
            hops.append(copy)

    @pl.when(zc == 0)
    def _():
        for i in range(4):
            hops[2 * i].start()

    def relay(i):
        @pl.when(zc == 0)
        def _():
            arrived(mid.at[i], mid_sem.at[i])
            hops[2 * i + 1].start()

    arrived(sibq, sibw_sem.at[1])
    for k in range(2):
        wq[2 * c + k, rows_of(q), :] = wq_in[2 * c + k] + sibq[k]

    xl, xr, xo = lax.rem(x + 3, 4), lax.rem(x + 1, 4), lax.rem(x + 2, 4)

    first_x = len(pending)
    rights = [post(wpart(i, 2 * x, 2), xp.at[i], right, first_x + i) for i in range(4)]
    lefts = [post(wpart(i, 2 * x, 2), xm.at[i], left, first_x + 4 + i) for i in range(4)]
    pending.extend((None, copy) for copy in rights + lefts)

    def x1_stage(i):
        @pl.when(zc == 0)
        def _():
            wall[near + i, rows_of(2 * x), :] = own[i]

        @pl.when(zc != 0)
        def _():
            arrived(wpart(i, 2 * x), yp.at[i])

        arrived(wpart(i, 2 * x + 1), ym.at[i])
        rights[i].start()
        lefts[i].start()

    def x2_stage(i):
        arrived(wpart(i, 2 * xl, 2), xp.at[i])
        send(wpart(i, 2 * xl), wpart(i, 2 * xl), xpp.at[i], right, z)
        arrived(wpart(i, 2 * xr, 2), xm.at[i])
        send(wpart(i, 2 * xr + 1), wpart(i, 2 * xr + 1), xmm.at[i], left, z)

    def x3_stage(i):
        arrived(wpart(i, 2 * xo), xpp.at[i])
        arrived(wpart(i, 2 * xo + 1), xmm.at[i])
        n = jnp.where(c == 0, i, i - 1)
        whole = wall.at[near + i]
        when = None if 0 < i < 3 else (c == 0 if i == 0 else c == 1)
        n = jnp.clip(n, 0, 2)
        send(whole, whole, ssib.at[n], sib, z, when)

    def qpart(k, nk, slot, n):
        return wq.at[pl.ds(2 * c + k, nk), rows_of(slot, n), :]

    row = 4 * y

    def q_row(step):
        return 4 * lax.rem(y + 8 + step, 8)

    def q_stage(s):
        if s == 0:
            own = qpart(0, 2, q, 1)
            send(own, own, qx.at[0], right, z)
            send(own, own, qx.at[1], left, z)
        elif s == 1:
            arrived(qpart(0, 2, row + xl, 1), qx.at[0])
            part = qpart(0, 1, row + xl, 1)
            send(part, part, qx.at[2], right, z)
            arrived(qpart(0, 2, row + xr, 1), qx.at[1])
            part = qpart(1, 1, row + xr, 1)
            send(part, part, qx.at[3], left, z)
        elif s == 2:
            arrived(qpart(0, 1, row + xo, 1), qx.at[2])
            arrived(qpart(1, 1, row + xo, 1), qx.at[3])
            block = qpart(0, 2, row, 4)
            for n in range(4):
                send(block, block, qy.at[n], near_y[n], z)
        elif s == 3:
            for n, step in enumerate((-1, 1, -2, 2)):
                arrived(qpart(0, 2, q_row(step), 4), qy.at[n])
            for n, (step, k, nk) in enumerate(((-1, 0, 2), (1, 0, 2), (-2, 0, 1), (2, 1, 1))):
                block = qpart(k, nk, q_row(step), 4)
                send(block, block, qy.at[4 + n], near_y[2 + n % 2], z)
        else:
            for n, (step, k, nk) in enumerate(((-3, 0, 2), (3, 0, 2), (4, 0, 1), (4, 1, 1))):
                arrived(qpart(k, nk, q_row(step), 4), qy.at[4 + n])
            both = wq.at[kinds]
            send(both, both, qsib, sib, z)

    def constants():
        gmat[...] = one_hot(twelfth(iota((C, C), 0)) == twelfth(iota((C, C), 1)))
        zero = jnp.zeros((32, 3 * C), BF)
        for s in range(4):
            act[s, 0:32, :] = zero
            act[s, 288:320, :] = zero
        def channel(place_in, k):
            slot = (place_in & 127) >> 4
            row_of = (y + 8 + jnp.where((slot & 1) == 0, k, jnp.where(k == 0, 4, -k))) & 7
            return 12 * (row_of * 4 + (slot >> 1)) + (place_in & 15)

        lane = iota((C, 128), 1)
        chan = channel(lane, zc)
        pick[...] = one_hot((iota((C, 128), 0) == chan) & ((lane & 15) < 12))
        part = iota((512, C), 0)
        chan = channel(part, part >> 7)
        pick_all[...] = one_hot((iota((512, C), 1) == chan) & ((part & 15) < 12))
        to, at = iota((128, 384), 0), iota((128, 384), 1)
        same = (to >> 4) == ((at & 127) >> 4)
        widen[...] = one_hot(same & ((at & 15) >= 12) & ((to & 15) == 4 * (at >> 7) + (at & 15) - 12))
        packed = iota((C, 512), 1)
        unpack[...] = one_hot((iota((C, 512), 0) == 12 * (packed >> 4) + (packed & 15)) & ((packed & 15) < 12))

    mine, halo = lat.at[pl.ds(2, 2)], lat.at[pl.ds(0, 2)]

    def frame_sum(s, mean):
        def step(i, total):
            v = lat[s, i].astype(F32)
            if mean is not None:
                v = v - mean
                v = v * v
            return total + v

        return jnp.sum(lax.fori_loop(0, 8, step, jnp.zeros((32, C), F32)), axis=0, keepdims=True)

    col = iota((32, C), 0)

    def activate(pair):
        frames = (2 * pair, 2 * pair + 1)
        means = group_means([frame_sum(s, None) for s in frames], gmat[...])
        variances = group_means([frame_sum(s, m) for s, m in zip(frames, means)], gmat[...])
        for s, m, var in zip(frames, means, variances):
            scale = lax.rsqrt(var + 1e-06)
            gain = gain1[...].reshape(1, C)
            empty = (c == 0) & (z < 4) & (q == 0) & (s < 2)

            def step(i, carry):
                v = (lat[s, i].astype(F32) - m) * scale * gain
                v = v / (1.0 + jnp.exp(-v))
                v = jnp.where(empty, 0.0, v)
                at = pl.ds(pl.multiple_of(32 * i + 32, 32), 32)
                act[s, at, 0:C] = jnp.where(col == 0, 0.0, pltpu.roll(v, 1, 0)).astype(BF)
                act[s, at, C : 2 * C] = v.astype(BF)
                act[s, at, 2 * C : 3 * C] = jnp.where(col == 31, 0.0, pltpu.roll(v, 31, 0)).astype(BF)
                return carry

            lax.fori_loop(0, 8, step, 0)

    def taps(ta, frames=(0, 1)):
        t, a = ta // 3, lax.rem(ta, 3)
        for j in frames:
            rows = pl.ds(pl.multiple_of(32 * a, 32), 256)
            acc[j] += dot_nt(act[j + t, rows, :], wall[ta])

    def own_taps(i):
        x3_stage(i)
        taps(near + i)

    def spread(e):
        units = wall[pl.ds(3 * e, 3)].reshape(384, 3 * C)
        wall[7 + e] = dot_nn(widen[...], units).astype(BF)

    q_stage(0)
    constants()
    arrived(gain1, gain_sem.at[0])
    arrived(gain2, gain_sem.at[1])
    relay(0)
    relay(1)
    relay(2)
    relay(3)
    x1_stage(0)
    x1_stage(1)
    q_stage(1)
    x1_stage(2)
    x2_stage(0)
    x1_stage(3)
    x2_stage(1)
    q_stage(2)
    x2_stage(2)
    arrived(mine, lat_sem.at[1])
    send(mine, halo, lat_sem.at[0], sib, z, c == 0)
    for j in range(2):
        acc[j] = dot_nn(lat[2 + j].reshape(256, C), pick[...])
    activate(1)
    x2_stage(3)
    q_stage(3)
    arrived(halo, lat_sem.at[0])
    activate(0)
    own_taps(0)
    own_taps(1)
    own_taps(2)
    own_taps(3)
    spread(c)
    taps(7 + c)

    def sib_unit(n):
        return jnp.where(c == 0, 4 + n, n)

    for n in range(3):
        arrived(wall.at[sib_unit(n)], ssib.at[n])
    spread(1 - c)

    for j in range(2):

        def sib_taps(n, carry):
            taps(jnp.where(n == 3, 8 - c, sib_unit(n)), (j,))
            return carry

        lax.fori_loop(0, 4, sib_taps, 0)
        thr_s[j] = acc[j].astype(BF)
        for k in (j, j + 2):
            dst = thr.at[:, pl.ds(pl.multiple_of(128 * zc, 128), 128)]
            send_or_keep(thr_s.at[j], dst, exsem.at[zc], tm, 4 * g + k)

    q_stage(4)
    arrived(wq.at[pl.ds(2 * (1 - c), 2)], qsib)
    w_value = dot_nn(unpack[...], wq[2]).astype(BF)
    w_out = dot_nn(unpack[...], wq[3]).astype(BF)
    for k in range(4):
        arrived(thr.at[:, pl.ds(128 * k, 128)], exsem.at[k])

    through = dot_nn(thr[...], pick_all[...])
    thrn[...] = through

    mean = group_means([jnp.sum(through, axis=0, keepdims=True)], gmat[...])[0]
    dev = through - mean
    var = group_means([jnp.sum(dev * dev, axis=0, keepdims=True)], gmat[...])[0]
    normed = (dev * lax.rsqrt(var + 1e-06) * gain2[...].reshape(1, C)).astype(BF)
    thr[:, 0:C] = normed

    mine_rows = pl.ds(pl.multiple_of(128 * half, 128), 128)
    queries = dot_nt(thr[mine_rows, 0:C], wq[0]).astype(BF)
    keys = dot_nt(normed, wq[1]).astype(BF)
    values = dot_nt(normed, w_value).astype(BF)
    scores = dot_nt(queries, keys) * (C ** -0.5)
    expon = jnp.exp(scores - jnp.max(scores, axis=1, keepdims=True))
    totals = jnp.sum(expon, axis=1, keepdims=True)
    attended = (dot_nn(expon.astype(BF), values) / totals).astype(BF)
    result = thrn[mine_rows, :] + dot_nt(attended, w_out)
    obuf[...] = result.astype(BF).reshape(4, 32, C)

    fr = 2 * c + fsel
    for k in range(4):
        send_or_keep(obuf.at[k], out_ref.at[fr], outsem.at[fr], 2 * q + g, 4 * half + k)
    for k in range(4):
        arrived(out_ref.at[k], outsem.at[k])

    for when, desc in pending:
        if when is None:
            desc.wait_send()
        else:
            pl.when(when)(desc.wait_send)


def body(latents, gain_one, conv_weight, gain_two, qkv_weight, out_weight):
    c = lax.rem(lax.axis_index("tm"), 2)
    taps = jnp.pad(conv_weight.transpose(2, 0, 1), ((0, 0), (0, 5), (0, 0)))
    proj = jnp.concatenate([qkv_weight.transpose(0, 2, 1), out_weight.T[None]], 0)

    def placed(w):
        low = jnp.pad(w, ((0, 0), (0, 10), (0, 0)))
        high = jnp.pad(w, ((0, 0), (6, 4), (0, 0)))
        return jnp.where(c == 0, low, high)

    vmem = pl.BlockSpec(memory_space=pltpu.VMEM)
    anywhere = pl.BlockSpec(memory_space=pl.ANY)
    dma = pltpu.SemaphoreType.DMA
    out = pl.pallas_call(
        kernel,
        out_shape=jax.ShapeDtypeStruct((4, 32, C), BF),
        in_specs=[anywhere, vmem, vmem, anywhere, anywhere],
        out_specs=vmem,
        scratch_shapes=[
            pltpu.VMEM((4, 8, 32, C), BF),
            pltpu.VMEM((7, 16, 3 * C), BF),
            pltpu.VMEM((4, 16, 3 * C), BF),
            pltpu.VMEM((2, 16, C), BF),
            pltpu.VMEM((4, 16, 3 * C), BF),
            pltpu.VMEM((4, 16, 3 * C), BF),
            pltpu.VMEM((9, 128, 3 * C), BF),
            pltpu.VMEM((4, 512, C), BF),
            pltpu.VMEM((4, 320, 3 * C), BF),
            pltpu.VMEM((2, 256, 128), F32),
            pltpu.VMEM((2, 256, 128), BF),
            pltpu.VMEM((256, 512), BF),
            pltpu.VMEM((256, C), F32),
            pltpu.VMEM((4, 32, C), BF),
            pltpu.VMEM((C, C), BF),
            pltpu.VMEM((C, 128), BF),
            pltpu.VMEM((512, C), BF),
            pltpu.VMEM((C, 512), BF),
            pltpu.VMEM((128, 384), BF),
            pltpu.VMEM((C,), F32),
            pltpu.VMEM((C,), F32),
            dma((NSEND,)), dma((2,)), dma((2,)), dma((5,)), dma((5,)), dma((5,)), dma((5,)), dma((5,)), dma((5,)),
            dma((4,)), dma((4,)), dma((8,)), dma, dma((4,)), dma((4,)), dma((2,)), dma((5,)),
        ],
        compiler_params=pltpu.CompilerParams(
            collective_id=0, has_side_effects=True, vmem_limit_bytes=40 * 1024 * 1024
        ),
        cost_estimate=pl.CostEstimate(flops=2 * 10**9, bytes_accessed=10**7, transcendentals=10**6),
    )(latents[:, 0], taps, placed(proj), gain_one, gain_two)
    return out[:, None]


def solution(mesh):
    in_specs = (
        P("tm", "rows", None, None),
        P(),
        P(None, None, "tm"),
        P(),
        P(None, None, "tm"),
        P(None, "tm"),
    )
    out_specs = P("tm", "rows", None, None)
    return jax.shard_map(body, mesh=mesh, in_specs=in_specs, out_specs=out_specs, check_vma=False)
```

```python
import jax
import jax.numpy as jnp
from jax import lax
from jax.experimental import pallas as pl
from jax.experimental.pallas import tpu as pltpu
from jax.sharding import PartitionSpec as P

C = 384
NX, NY, NZ = 4, 8, 8
BF = jnp.bfloat16
F32 = jnp.float32
MESH = pl.DeviceIdType.MESH
NSEND = 96


def iota(shape, dim):
    return lax.broadcasted_iota(jnp.int32, shape, dim)


def twelfth(i):
    return (i * 43691) >> 19


def one_hot(mask):
    return jnp.where(mask, 1.0, 0.0).astype(BF)


def dot_nn(a, b):
    return lax.dot_general(a, b, (((1,), (0,)), ((), ())), preferred_element_type=F32)


def dot_nt(a, b):
    return lax.dot_general(a, b, (((1,), (1,)), ((), ())), preferred_element_type=F32)


def group_means(sums, gmat):
    rows = iota((16, C), 0)
    stack = jnp.zeros((16, C), F32)
    for n, s in enumerate(sums):
        high = s.astype(BF).astype(F32)
        rest = s - high
        mid = rest.astype(BF).astype(F32)
        for k, part in enumerate((high, mid, rest - mid)):
            stack = jnp.where(rows == 3 * n + k, part, stack)
    res = dot_nn(stack.astype(BF), gmat)
    out = []
    for n in range(len(sums)):
        total = res[3 * n : 3 * n + 1] + res[3 * n + 1 : 3 * n + 2] + res[3 * n + 2 : 3 * n + 3]
        out.append(total * (1.0 / (12 * 256)))
    return out


def kernel(
    lat_in, wc_in, wq_in, gain1_in, gain2_in, out_ref,
    lat, wc, sibc, sibq, own, mid, wall, qpad, wq, act, acc, thr_s, thr, thrn, obuf, gmat, pick, pick_all, widen, gain1, gain2,
    sends, lat_sem, sibw_sem, yp, ym, xp, xm, xpp, xmm, ssib, qx, qy, qsib, exsem, outsem, gain_sem, mid_sem,
):
    tm = lax.axis_index("tm")
    z = lax.axis_index("rows")
    c = lax.rem(tm, 2)
    q = tm // 2
    x = lax.rem(q, NX)
    y = q // NX
    g = z // 4
    zc = lax.rem(z, 4)
    half = zc // 2
    fsel = lax.rem(zc, 2)

    pending = []

    def place(yy, xx, core):
        return (lax.rem(yy + NY, NY) * NX + lax.rem(xx + NX, NX)) * 2 + core

    def send(src, dst, rsem, to_tm, to_z, when=None):
        d = pltpu.make_async_remote_copy(
            src_ref=src, dst_ref=dst, send_sem=sends.at[len(pending)], recv_sem=rsem,
            device_id=(to_tm, to_z), device_id_type=MESH,
        )
        if when is None:
            d.start()
        else:
            pl.when(when)(d.start)
        pending.append((when, d))

    def send_or_keep(src, dst, rsem, to_tm, to_z):
        here = jnp.logical_and(to_tm == tm, to_z == z)
        send(src, dst, rsem, to_tm, to_z, jnp.logical_not(here))
        pl.when(here)(pltpu.make_async_copy(src, dst, rsem).start)

    def arrived(ref, sem):
        pltpu.make_async_copy(ref, ref, sem).wait()

    for k, (src, dst) in enumerate(((gain1_in, gain1), (gain2_in, gain2))):
        pltpu.make_async_copy(src, dst, gain_sem.at[k]).start()

    barrier = pltpu.get_barrier_semaphore()

    def sends_to(c0, z0, c1, z1):
        a = z1 // 4 == c0
        a = a | ((c0 == 0) & (c1 == 0) & (z1 // 4 == 1))
        a = a | (z1 == z0)
        a = a | ((c1 == c0) & (z1 // 4 == z0 // 4))
        a = a | ((c1 == z0 // 4) & (z1 // 4 == lax.rem(z0, 4) // 2))
        return a & jnp.logical_not((c0 == c1) & (z0 == z1))

    def greet(i, count):
        co, zo = i // NZ, lax.rem(i, NZ)

        @pl.when(sends_to(co, zo, c, z))
        def _():
            pl.semaphore_signal(barrier, inc=1, device_id=(2 * q + co, zo), device_id_type=MESH)

        return count + jnp.where(sends_to(c, z, co, zo), 1, 0)

    count = lax.fori_loop(0, 2 * NZ, greet, jnp.int32(0))
    right, left = place(y, x + 1, c), place(y, x - 1, c)
    near_y = [place(y + step, x, c) for step in (1, -1, 2, -2)]
    for other in [right, left] + near_y:
        pl.semaphore_signal(barrier, inc=1, device_id=(other, z), device_id_type=MESH)

    @pl.when(zc == 3)
    def _():
        for step in (3, -3):
            pl.semaphore_signal(barrier, inc=1, device_id=(place(y + step, x, c), z), device_id_type=MESH)

    prev_q = lax.rem(q + 31, 32)

    @pl.when((c == 0) & (z < 4))
    def _():
        def halo_greet(r, carry):
            pl.semaphore_signal(barrier, inc=1, device_id=(2 * prev_q + 1, r), device_id_type=MESH)
            return carry

        lax.fori_loop(0, NZ, halo_greet, 0)

    raw = wc_in[...].reshape(192, C)
    r16, unit = iota((112, 192), 0) & 15, iota((112, 192), 0) >> 4
    third = twelfth(4 * unit)
    tail = r16 >= 12
    chan_of = jnp.where(tail, 4 * (unit - 3 * third) + r16 - 12, r16)
    tap_row = jnp.where(tail, 7 + third, unit)
    shard_row, tap = iota((112, 192), 1) >> 5, iota((112, 192), 1) & 31
    for b in range(3):
        wanted = (chan_of == 6 * c + shard_row) & (tap == 3 * tap_row + b) & (tap_row < 9)
        wc[:, :, b * C : (b + 1) * C] = dot_nn(one_hot(wanted), raw).astype(BF).reshape(7, 16, C)

    pl.semaphore_wait(barrier, count + 6 + 4 * c + jnp.where(zc == 3, 2, 0))

    sib = 2 * q + 1 - c
    far_row = jnp.where(zc == 0, 4, -zc)

    near, far = 3 * c, 3 * (1 - c)
    send(wc.at[pl.ds(far, 4)], sibc, sibw_sem.at[0], sib, z)
    send(wq_in.at[pl.ds(2 * (1 - c), 2)], sibq, sibw_sem.at[1], sib, z)

    q_halo = lax.rem(q + c, 32)
    for k in range(4):
        send_or_keep(lat_in.at[pl.ds(0, 2)], lat.at[pl.ds(2, 2), z], lat_sem.at[1], 2 * q, 4 * c + k)
        send_or_keep(lat_in.at[pl.ds(2, 2)], lat.at[pl.ds(2, 2), z], lat_sem.at[1], 2 * q + 1, 4 * c + k)
        send_or_keep(lat_in.at[pl.ds(2, 2)], lat.at[pl.ds(0, 2), z], lat_sem.at[0], 2 * q_halo, 4 * (1 - c) + k)

    def rows_of(slot, n=1):
        return pl.ds(pl.multiple_of(16 * slot, 16), 16 * n)

    kinds = pl.ds(2 * c, 2)

    def wpart(i, slot, n=1):
        return wall.at[near + i, rows_of(slot, n), :]

    def post(src, rsem, to_tm, index):
        return pltpu.make_async_remote_copy(
            src_ref=src, dst_ref=src, send_sem=sends.at[index], recv_sem=rsem,
            device_id=(to_tm, z), device_id_type=MESH,
        )

    to_first, to_second = place(y - zc, x, c), place(y - far_row, x, c)
    arrived(sibc, sibw_sem.at[0])
    for i in range(4):
        own[i] = wc[near + i] + sibc[i]
        for h, (to, sem) in enumerate(((to_first, yp), (to_second, ym))):
            copy = pltpu.make_async_remote_copy(
                src_ref=own.at[i], dst_ref=wpart(i, 2 * x + h), send_sem=sends.at[len(pending)],
                recv_sem=sem.at[i], device_id=(to, z), device_id_type=MESH,
            )
            pl.when(zc != 0)(copy.start)
            pending.append((zc != 0, copy))

    hops = []
    for i in range(4):
        for src, dst, sem in ((own.at[i], mid.at[i], mid_sem), (mid.at[i], wpart(i, 2 * x + 1), ym)):
            copy = pltpu.make_async_remote_copy(
                src_ref=src, dst_ref=dst, send_sem=sends.at[len(pending)], recv_sem=sem.at[i],
                device_id=(near_y[2 + i % 2], z), device_id_type=MESH,
            )
            pending.append((zc == 0, copy))
            hops.append(copy)

    @pl.when(zc == 0)
    def _():
        for i in range(4):
            hops[2 * i].start()

    def relay(i):
        @pl.when(zc == 0)
        def _():
            arrived(mid.at[i], mid_sem.at[i])
            hops[2 * i + 1].start()

    arrived(sibq, sibw_sem.at[1])
    for k in range(2):
        qpad[k, rows_of(x), :] = wq_in[2 * c + k] + sibq[k]

    xl, xr, xo = lax.rem(x + 3, 4), lax.rem(x + 1, 4), lax.rem(x + 2, 4)

    first_x = len(pending)
    rights = [post(wpart(i, 2 * x, 2), xp.at[i], right, first_x + i) for i in range(4)]
    lefts = [post(wpart(i, 2 * x, 2), xm.at[i], left, first_x + 4 + i) for i in range(4)]
    pending.extend((None, copy) for copy in rights + lefts)

    def x1_stage(i):
        @pl.when(zc == 0)
        def _():
            wall[near + i, rows_of(2 * x), :] = own[i]

        @pl.when(zc != 0)
        def _():
            arrived(wpart(i, 2 * x), yp.at[i])

        arrived(wpart(i, 2 * x + 1), ym.at[i])
        rights[i].start()
        lefts[i].start()

    def x2_stage(i):
        arrived(wpart(i, 2 * xl, 2), xp.at[i])
        send(wpart(i, 2 * xl), wpart(i, 2 * xl), xpp.at[i], right, z)
        arrived(wpart(i, 2 * xr, 2), xm.at[i])
        send(wpart(i, 2 * xr + 1), wpart(i, 2 * xr + 1), xmm.at[i], left, z)

    def x3_stage(i):
        arrived(wpart(i, 2 * xo), xpp.at[i])
        arrived(wpart(i, 2 * xo + 1), xmm.at[i])
        n = jnp.where(c == 0, i, i - 1)
        whole = wall.at[near + i]
        when = None if 0 < i < 3 else (c == 0 if i == 0 else c == 1)
        n = jnp.clip(n, 0, 2)
        send(whole, whole, ssib.at[n], sib, z, when)

    def xpart(k, nk, xx):
        return qpad.at[pl.ds(k, nk), rows_of(xx), :]

    def ypart(k, nk, step):
        yy = lax.rem(y + 8 + step, 8)
        return wq.at[pl.ds(2 * c + k, nk), pl.ds(pl.multiple_of(48 * yy, 16), 48), :]

    def q_stage(s):
        if s == 0:
            piece = xpart(0, 2, x)
            send(piece, piece, qx.at[0], right, z)
            send(piece, piece, qx.at[1], left, z)
        elif s == 1:
            arrived(xpart(0, 2, xl), qx.at[0])
            part = xpart(0, 1, xl)
            send(part, part, qx.at[2], right, z)
            arrived(xpart(0, 2, xr), qx.at[1])
            part = xpart(1, 1, xr)
            send(part, part, qx.at[3], left, z)
        elif s == 2:
            arrived(xpart(0, 1, xo), qx.at[2])
            arrived(xpart(1, 1, xo), qx.at[3])
            wide = iota((48, 64), 0)
            tight = one_hot(iota((48, 64), 1) == wide + 4 * twelfth(wide))
            for k in range(2):
                wq[2 * c + k, pl.ds(pl.multiple_of(48 * y, 16), 48), :] = dot_nn(tight, qpad[k]).astype(BF)
            block = ypart(0, 2, 0)
            for n in range(4):
                send(block, block, qy.at[n], near_y[n], z)
        elif s == 3:
            for n, step in enumerate((-1, 1, -2, 2)):
                arrived(ypart(0, 2, step), qy.at[n])
            for n, (step, k, nk) in enumerate(((-1, 0, 2), (1, 0, 2), (-2, 0, 1), (2, 1, 1))):
                block = ypart(k, nk, step)
                send(block, block, qy.at[4 + n], near_y[2 + n % 2], z)
        else:
            for n, (step, k, nk) in enumerate(((-3, 0, 2), (3, 0, 2), (4, 0, 1), (4, 1, 1))):
                arrived(ypart(k, nk, step), qy.at[4 + n])
            both = wq.at[kinds]
            send(both, both, qsib, sib, z)

    def constants():
        gmat[...] = one_hot(twelfth(iota((C, C), 0)) == twelfth(iota((C, C), 1)))
        zero = jnp.zeros((32, 3 * C), BF)
        for s in range(4):
            act[s, 0:32, :] = zero
            act[s, 288:320, :] = zero
        def channel(place_in, k):
            slot = (place_in & 127) >> 4
            row_of = (y + 8 + jnp.where((slot & 1) == 0, k, jnp.where(k == 0, 4, -k))) & 7
            return 12 * (row_of * 4 + (slot >> 1)) + (place_in & 15)

        lane = iota((C, 128), 1)
        chan = channel(lane, zc)
        pick[...] = one_hot((iota((C, 128), 0) == chan) & ((lane & 15) < 12))
        part = iota((512, C), 0)
        chan = channel(part, part >> 7)
        pick_all[...] = one_hot((iota((512, C), 1) == chan) & ((part & 15) < 12))
        to, at = iota((128, 384), 0), iota((128, 384), 1)
        same = (to >> 4) == ((at & 127) >> 4)
        widen[...] = one_hot(same & ((at & 15) >= 12) & ((to & 15) == 4 * (at >> 7) + (at & 15) - 12))

    mine, halo = lat.at[pl.ds(2, 2)], lat.at[pl.ds(0, 2)]

    def frame_sum(s, mean):
        def step(i, total):
            v = lat[s, i].astype(F32)
            if mean is not None:
                v = v - mean
                v = v * v
            return total + v

        return jnp.sum(lax.fori_loop(0, 8, step, jnp.zeros((32, C), F32)), axis=0, keepdims=True)

    col = iota((32, C), 0)

    def activate(pair):
        frames = (2 * pair, 2 * pair + 1)
        means = group_means([frame_sum(s, None) for s in frames], gmat[...])
        variances = group_means([frame_sum(s, m) for s, m in zip(frames, means)], gmat[...])
        for s, m, var in zip(frames, means, variances):
            scale = lax.rsqrt(var + 1e-06)
            gain = gain1[...].reshape(1, C)
            empty = (c == 0) & (z < 4) & (q == 0) & (s < 2)

            def step(i, carry):
                v = (lat[s, i].astype(F32) - m) * scale * gain
                v = v / (1.0 + jnp.exp(-v))
                v = jnp.where(empty, 0.0, v)
                at = pl.ds(pl.multiple_of(32 * i + 32, 32), 32)
                act[s, at, 0:C] = jnp.where(col == 0, 0.0, pltpu.roll(v, 1, 0)).astype(BF)
                act[s, at, C : 2 * C] = v.astype(BF)
                act[s, at, 2 * C : 3 * C] = jnp.where(col == 31, 0.0, pltpu.roll(v, 31, 0)).astype(BF)
                return carry

            lax.fori_loop(0, 8, step, 0)

    def taps(ta, frames=(0, 1)):
        t, a = ta // 3, lax.rem(ta, 3)
        for j in frames:
            rows = pl.ds(pl.multiple_of(32 * a, 32), 256)
            acc[j] += dot_nt(act[j + t, rows, :], wall[ta])

    def own_taps(i):
        x3_stage(i)
        taps(near + i)

    def spread(e):
        units = wall[pl.ds(3 * e, 3)].reshape(384, 3 * C)
        wall[7 + e] = dot_nn(widen[...], units).astype(BF)

    q_stage(0)
    constants()
    arrived(gain1, gain_sem.at[0])
    arrived(gain2, gain_sem.at[1])
    relay(0)
    relay(1)
    relay(2)
    relay(3)
    x1_stage(0)
    x1_stage(1)
    q_stage(1)
    x1_stage(2)
    x2_stage(0)
    x1_stage(3)
    q_stage(2)
    x2_stage(1)
    x2_stage(2)
    arrived(mine, lat_sem.at[1])
    send(mine, halo, lat_sem.at[0], sib, z, c == 0)
    for j in range(2):
        acc[j] = dot_nn(lat[2 + j].reshape(256, C), pick[...])
    activate(1)
    x2_stage(3)
    arrived(halo, lat_sem.at[0])
    activate(0)
    own_taps(0)
    q_stage(3)
    own_taps(1)
    own_taps(2)
    own_taps(3)
    spread(c)
    taps(7 + c)

    def sib_unit(n):
        return jnp.where(c == 0, 4 + n, n)

    for n in range(3):
        arrived(wall.at[sib_unit(n)], ssib.at[n])
    spread(1 - c)

    for j in range(2):

        def sib_taps(n, carry):
            taps(jnp.where(n == 3, 8 - c, sib_unit(n)), (j,))
            return carry

        lax.fori_loop(0, 4, sib_taps, 0)
        thr_s[j] = acc[j].astype(BF)
        for k in (j, j + 2):
            dst = thr.at[:, pl.ds(pl.multiple_of(128 * zc, 128), 128)]
            send_or_keep(thr_s.at[j], dst, exsem.at[zc], tm, 4 * g + k)

    q_stage(4)
    for k in range(4):
        arrived(thr.at[:, pl.ds(128 * k, 128)], exsem.at[k])

    through = dot_nn(thr[...], pick_all[...])
    thrn[...] = through

    mean = group_means([jnp.sum(through, axis=0, keepdims=True)], gmat[...])[0]
    dev = through - mean
    var = group_means([jnp.sum(dev * dev, axis=0, keepdims=True)], gmat[...])[0]
    normed = (dev * lax.rsqrt(var + 1e-06) * gain2[...].reshape(1, C)).astype(BF)
    thr[:, 0:C] = normed

    arrived(wq.at[pl.ds(2 * (1 - c), 2)], qsib)
    mine_rows = pl.ds(pl.multiple_of(128 * half, 128), 128)
    queries = dot_nt(thr[mine_rows, 0:C], wq[0]).astype(BF)
    keys = dot_nt(normed, wq[1]).astype(BF)
    values = dot_nt(normed, wq[2]).astype(BF)
    scores = dot_nt(queries, keys) * (C ** -0.5)
    expon = jnp.exp(scores - jnp.max(scores, axis=1, keepdims=True))
    totals = jnp.sum(expon, axis=1, keepdims=True)
    attended = (dot_nn(expon.astype(BF), values) / totals).astype(BF)
    result = thrn[mine_rows, :] + dot_nt(attended, wq[3])
    obuf[...] = result.astype(BF).reshape(4, 32, C)

    fr = 2 * c + fsel
    for k in range(4):
        send_or_keep(obuf.at[k], out_ref.at[fr], outsem.at[fr], 2 * q + g, 4 * half + k)
    for k in range(4):
        arrived(out_ref.at[k], outsem.at[k])

    for when, desc in pending:
        if when is None:
            desc.wait_send()
        else:
            pl.when(when)(desc.wait_send)


def body(latents, gain_one, conv_weight, gain_two, qkv_weight, out_weight):
    c = lax.rem(lax.axis_index("tm"), 2)
    taps = jnp.pad(conv_weight.transpose(2, 0, 1), ((0, 0), (0, 5), (0, 0)))
    proj = jnp.concatenate([qkv_weight.transpose(0, 2, 1), out_weight.T[None]], 0)

    def placed(w):
        low = jnp.pad(w, ((0, 0), (0, 10), (0, 0)))
        high = jnp.pad(w, ((0, 0), (6, 4), (0, 0)))
        return jnp.where(c == 0, low, high)

    vmem = pl.BlockSpec(memory_space=pltpu.VMEM)
    anywhere = pl.BlockSpec(memory_space=pl.ANY)
    dma = pltpu.SemaphoreType.DMA
    out = pl.pallas_call(
        kernel,
        out_shape=jax.ShapeDtypeStruct((4, 32, C), BF),
        in_specs=[anywhere, vmem, vmem, anywhere, anywhere],
        out_specs=vmem,
        scratch_shapes=[
            pltpu.VMEM((4, 8, 32, C), BF),
            pltpu.VMEM((7, 16, 3 * C), BF),
            pltpu.VMEM((4, 16, 3 * C), BF),
            pltpu.VMEM((2, 16, C), BF),
            pltpu.VMEM((4, 16, 3 * C), BF),
            pltpu.VMEM((4, 16, 3 * C), BF),
            pltpu.VMEM((9, 128, 3 * C), BF),
            pltpu.VMEM((2, 64, C), BF),
            pltpu.VMEM((4, C, C), BF),
            pltpu.VMEM((4, 320, 3 * C), BF),
            pltpu.VMEM((2, 256, 128), F32),
            pltpu.VMEM((2, 256, 128), BF),
            pltpu.VMEM((256, 512), BF),
            pltpu.VMEM((256, C), F32),
            pltpu.VMEM((4, 32, C), BF),
            pltpu.VMEM((C, C), BF),
            pltpu.VMEM((C, 128), BF),
            pltpu.VMEM((512, C), BF),
            pltpu.VMEM((128, 384), BF),
            pltpu.VMEM((C,), F32),
            pltpu.VMEM((C,), F32),
            dma((NSEND,)), dma((2,)), dma((2,)), dma((5,)), dma((5,)), dma((5,)), dma((5,)), dma((5,)), dma((5,)),
            dma((4,)), dma((4,)), dma((8,)), dma, dma((4,)), dma((4,)), dma((2,)), dma((5,)),
        ],
        compiler_params=pltpu.CompilerParams(
            collective_id=0, has_side_effects=True, vmem_limit_bytes=40 * 1024 * 1024
        ),
        cost_estimate=pl.CostEstimate(flops=2 * 10**9, bytes_accessed=10**7, transcendentals=10**6),
    )(latents[:, 0], taps, placed(proj), gain_one, gain_two)
    return out[:, None]


def solution(mesh):
    in_specs = (
        P("tm", "rows", None, None),
        P(),
        P(None, None, "tm"),
        P(),
        P(None, None, "tm"),
        P(None, "tm"),
    )
    out_specs = P("tm", "rows", None, None)
    return jax.shard_map(body, mesh=mesh, in_specs=in_specs, out_specs=out_specs, check_vma=False)
```

```python
import jax
import jax.numpy as jnp
from jax import lax
from jax.experimental import pallas as pl
from jax.experimental.pallas import tpu as pltpu
from jax.sharding import PartitionSpec as P

C = 384
NX, NY, NZ = 4, 8, 8
BF = jnp.bfloat16
F32 = jnp.float32
MESH = pl.DeviceIdType.MESH
NSEND = 96


def iota(shape, dim):
    return lax.broadcasted_iota(jnp.int32, shape, dim)


def twelfth(i):
    return (i * 43691) >> 19


def one_hot(mask):
    return jnp.where(mask, 1.0, 0.0).astype(BF)


def dot_nn(a, b):
    return lax.dot_general(a, b, (((1,), (0,)), ((), ())), preferred_element_type=F32)


def dot_nt(a, b):
    return lax.dot_general(a, b, (((1,), (1,)), ((), ())), preferred_element_type=F32)


def group_means(sums, gmat):
    rows = iota((16, C), 0)
    stack = jnp.zeros((16, C), F32)
    for n, s in enumerate(sums):
        high = s.astype(BF).astype(F32)
        rest = s - high
        mid = rest.astype(BF).astype(F32)
        for k, part in enumerate((high, mid, rest - mid)):
            stack = jnp.where(rows == 3 * n + k, part, stack)
    res = dot_nn(stack.astype(BF), gmat)
    out = []
    for n in range(len(sums)):
        total = res[3 * n : 3 * n + 1] + res[3 * n + 1 : 3 * n + 2] + res[3 * n + 2 : 3 * n + 3]
        out.append(total * (1.0 / (12 * 256)))
    return out


def kernel(
    lat_in, wc_in, wq_in, gain1_in, gain2_in, out_ref,
    lat, wc, sibc, sibq, own, mid, wall, qpad, wq, act, acc, thr_s, thr, thrn, obuf, gmat, pick, pick_all, widen, gain1, gain2,
    sends, lat_sem, sibw_sem, yp, ym, xp, xm, xpp, xmm, ssib, qx, qy, qsib, exsem, outsem, gain_sem, mid_sem,
):
    tm = lax.axis_index("tm")
    z = lax.axis_index("rows")
    c = lax.rem(tm, 2)
    q = tm // 2
    x = lax.rem(q, NX)
    y = q // NX
    g = z // 4
    zc = lax.rem(z, 4)
    half = zc // 2
    fsel = lax.rem(zc, 2)

    pending = []

    def place(yy, xx, core):
        return (lax.rem(yy + NY, NY) * NX + lax.rem(xx + NX, NX)) * 2 + core

    def send(src, dst, rsem, to_tm, to_z, when=None):
        d = pltpu.make_async_remote_copy(
            src_ref=src, dst_ref=dst, send_sem=sends.at[len(pending)], recv_sem=rsem,
            device_id=(to_tm, to_z), device_id_type=MESH,
        )
        if when is None:
            d.start()
        else:
            pl.when(when)(d.start)
        pending.append((when, d))

    def send_or_keep(src, dst, rsem, to_tm, to_z):
        here = jnp.logical_and(to_tm == tm, to_z == z)
        send(src, dst, rsem, to_tm, to_z, jnp.logical_not(here))
        pl.when(here)(pltpu.make_async_copy(src, dst, rsem).start)

    def arrived(ref, sem):
        pltpu.make_async_copy(ref, ref, sem).wait()

    for k, (src, dst) in enumerate(((gain1_in, gain1), (gain2_in, gain2))):
        pltpu.make_async_copy(src, dst, gain_sem.at[k]).start()

    barrier = pltpu.get_barrier_semaphore()

    def sends_to(c0, z0, c1, z1):
        a = z1 // 4 == c0
        a = a | ((c0 == 0) & (c1 == 0) & (z1 // 4 == 1))
        a = a | (z1 == z0)
        a = a | ((c1 == c0) & (z1 // 4 == z0 // 4))
        a = a | ((c1 == z0 // 4) & (z1 // 4 == lax.rem(z0, 4) // 2))
        return a & jnp.logical_not((c0 == c1) & (z0 == z1))

    def greet(i, count):
        co, zo = i // NZ, lax.rem(i, NZ)

        @pl.when(sends_to(co, zo, c, z))
        def _():
            pl.semaphore_signal(barrier, inc=1, device_id=(2 * q + co, zo), device_id_type=MESH)

        return count + jnp.where(sends_to(c, z, co, zo), 1, 0)

    count = lax.fori_loop(0, 2 * NZ, greet, jnp.int32(0))
    right, left = place(y, x + 1, c), place(y, x - 1, c)
    near_y = [place(y + step, x, c) for step in (1, -1, 2, -2)]
    for other in [right, left] + near_y:
        pl.semaphore_signal(barrier, inc=1, device_id=(other, z), device_id_type=MESH)

    @pl.when(zc == 3)
    def _():
        for step in (3, -3):
            pl.semaphore_signal(barrier, inc=1, device_id=(place(y + step, x, c), z), device_id_type=MESH)

    prev_q = lax.rem(q + 31, 32)

    @pl.when((c == 0) & (z < 4))
    def _():
        def halo_greet(r, carry):
            pl.semaphore_signal(barrier, inc=1, device_id=(2 * prev_q + 1, r), device_id_type=MESH)
            return carry

        lax.fori_loop(0, NZ, halo_greet, 0)

    raw = wc_in[...].reshape(192, C)
    r16, unit = iota((112, 192), 0) & 15, iota((112, 192), 0) >> 4
    third = twelfth(4 * unit)
    tail = r16 >= 12
    chan_of = jnp.where(tail, 4 * (unit - 3 * third) + r16 - 12, r16)
    tap_row = jnp.where(tail, 7 + third, unit)
    shard_row, tap = iota((112, 192), 1) >> 5, iota((112, 192), 1) & 31
    for b in range(3):
        wanted = (chan_of == 6 * c + shard_row) & (tap == 3 * tap_row + b) & (tap_row < 9)
        wc[:, :, b * C : (b + 1) * C] = dot_nn(one_hot(wanted), raw).astype(BF).reshape(7, 16, C)

    pl.semaphore_wait(barrier, count + 6 + 4 * c + jnp.where(zc == 3, 2, 0))

    sib = 2 * q + 1 - c
    far_row = jnp.where(zc == 0, 4, -zc)

    near, far = 3 * c, 3 * (1 - c)
    for i in range(4):
        send(wc.at[far + i], sibc.at[i], sibw_sem.at[i], sib, z)
    send(wq_in.at[pl.ds(2 * (1 - c), 2)], sibq, sibw_sem.at[4], sib, z)

    def rows_of(slot, n=1):
        return pl.ds(pl.multiple_of(16 * slot, 16), 16 * n)

    kinds = pl.ds(2 * c, 2)

    def wpart(i, slot, n=1):
        return wall.at[near + i, rows_of(slot, n), :]

    def post(src, rsem, to_tm, index):
        return pltpu.make_async_remote_copy(
            src_ref=src, dst_ref=src, send_sem=sends.at[index], recv_sem=rsem,
            device_id=(to_tm, z), device_id_type=MESH,
        )

    to_first, to_second = place(y - zc, x, c), place(y - far_row, x, c)
    for i in range(4):
        arrived(sibc.at[i], sibw_sem.at[i])
        own[i] = wc[near + i] + sibc[i]
        for h, (to, sem) in enumerate(((to_first, yp), (to_second, ym))):
            copy = pltpu.make_async_remote_copy(
                src_ref=own.at[i], dst_ref=wpart(i, 2 * x + h), send_sem=sends.at[len(pending)],
                recv_sem=sem.at[i], device_id=(to, z), device_id_type=MESH,
            )
            pl.when(zc != 0)(copy.start)
            pending.append((zc != 0, copy))

    hops = []
    for i in range(4):
        for src, dst, sem in ((own.at[i], mid.at[i], mid_sem), (mid.at[i], wpart(i, 2 * x + 1), ym)):
            copy = pltpu.make_async_remote_copy(
                src_ref=src, dst_ref=dst, send_sem=sends.at[len(pending)], recv_sem=sem.at[i],
                device_id=(near_y[2 + i % 2], z), device_id_type=MESH,
            )
            pending.append((zc == 0, copy))
            hops.append(copy)

    @pl.when(zc == 0)
    def _():
        for i in range(4):
            hops[2 * i].start()

    q_halo = lax.rem(q + c, 32)
    for k in range(4):
        send_or_keep(lat_in.at[pl.ds(0, 2)], lat.at[pl.ds(2, 2), z], lat_sem.at[1], 2 * q, 4 * c + k)
        send_or_keep(lat_in.at[pl.ds(2, 2)], lat.at[pl.ds(2, 2), z], lat_sem.at[1], 2 * q + 1, 4 * c + k)
        send_or_keep(lat_in.at[pl.ds(2, 2)], lat.at[pl.ds(0, 2), z], lat_sem.at[0], 2 * q_halo, 4 * (1 - c) + k)

    def relay(i):
        @pl.when(zc == 0)
        def _():
            arrived(mid.at[i], mid_sem.at[i])
            hops[2 * i + 1].start()

    arrived(sibq, sibw_sem.at[4])
    for k in range(2):
        qpad[k, rows_of(x), :] = wq_in[2 * c + k] + sibq[k]

    xl, xr, xo = lax.rem(x + 3, 4), lax.rem(x + 1, 4), lax.rem(x + 2, 4)

    first_x = len(pending)
    rights = [post(wpart(i, 2 * x, 2), xp.at[i], right, first_x + i) for i in range(4)]
    lefts = [post(wpart(i, 2 * x, 2), xm.at[i], left, first_x + 4 + i) for i in range(4)]
    pending.extend((None, copy) for copy in rights + lefts)

    def x1_stage(i):
        @pl.when(zc == 0)
        def _():
            wall[near + i, rows_of(2 * x), :] = own[i]

        @pl.when(zc != 0)
        def _():
            arrived(wpart(i, 2 * x), yp.at[i])

        arrived(wpart(i, 2 * x + 1), ym.at[i])
        rights[i].start()
        lefts[i].start()

    def x2_stage(i):
        arrived(wpart(i, 2 * xl, 2), xp.at[i])
        send(wpart(i, 2 * xl), wpart(i, 2 * xl), xpp.at[i], right, z)
        arrived(wpart(i, 2 * xr, 2), xm.at[i])
        send(wpart(i, 2 * xr + 1), wpart(i, 2 * xr + 1), xmm.at[i], left, z)

    def x3_stage(i):
        arrived(wpart(i, 2 * xo), xpp.at[i])
        arrived(wpart(i, 2 * xo + 1), xmm.at[i])
        n = jnp.where(c == 0, i, i - 1)
        whole = wall.at[near + i]
        when = None if 0 < i < 3 else (c == 0 if i == 0 else c == 1)
        n = jnp.clip(n, 0, 2)
        send(whole, whole, ssib.at[n], sib, z, when)

    def xpart(k, nk, xx):
        return qpad.at[pl.ds(k, nk), rows_of(xx), :]

    def ypart(k, nk, step):
        yy = lax.rem(y + 8 + step, 8)
        return wq.at[pl.ds(2 * c + k, nk), pl.ds(pl.multiple_of(48 * yy, 16), 48), :]

    def q_stage(s):
        if s == 0:
            piece = xpart(0, 2, x)
            send(piece, piece, qx.at[0], right, z)
            send(piece, piece, qx.at[1], left, z)
        elif s == 1:
            arrived(xpart(0, 2, xl), qx.at[0])
            part = xpart(0, 1, xl)
            send(part, part, qx.at[2], right, z)
            arrived(xpart(0, 2, xr), qx.at[1])
            part = xpart(1, 1, xr)
            send(part, part, qx.at[3], left, z)
        elif s == 2:
            arrived(xpart(0, 1, xo), qx.at[2])
            arrived(xpart(1, 1, xo), qx.at[3])
            wide = iota((48, 64), 0)
            tight = one_hot(iota((48, 64), 1) == wide + 4 * twelfth(wide))
            for k in range(2):
                wq[2 * c + k, pl.ds(pl.multiple_of(48 * y, 16), 48), :] = dot_nn(tight, qpad[k]).astype(BF)
            block = ypart(0, 2, 0)
            for n in range(4):
                send(block, block, qy.at[n], near_y[n], z)
        elif s == 3:
            for n, step in enumerate((-1, 1, -2, 2)):
                arrived(ypart(0, 2, step), qy.at[n])
            for n, (step, k, nk) in enumerate(((-1, 0, 2), (1, 0, 2), (-2, 0, 1), (2, 1, 1))):
                block = ypart(k, nk, step)
                send(block, block, qy.at[4 + n], near_y[2 + n % 2], z)
        else:
            for n, (step, k, nk) in enumerate(((-3, 0, 2), (3, 0, 2), (4, 0, 1), (4, 1, 1))):
                arrived(ypart(k, nk, step), qy.at[4 + n])
            both = wq.at[kinds]
            send(both, both, qsib, sib, z)

    def constants():
        gmat[...] = one_hot(twelfth(iota((C, C), 0)) == twelfth(iota((C, C), 1)))
        zero = jnp.zeros((32, 3 * C), BF)
        for s in range(4):
            act[s, 0:32, :] = zero
            act[s, 288:320, :] = zero
        def channel(place_in, k):
            slot = (place_in & 127) >> 4
            row_of = (y + 8 + jnp.where((slot & 1) == 0, k, jnp.where(k == 0, 4, -k))) & 7
            return 12 * (row_of * 4 + (slot >> 1)) + (place_in & 15)

        lane = iota((C, 128), 1)
        chan = channel(lane, zc)
        pick[...] = one_hot((iota((C, 128), 0) == chan) & ((lane & 15) < 12))
        part = iota((512, C), 0)
        chan = channel(part, part >> 7)
        pick_all[...] = one_hot((iota((512, C), 1) == chan) & ((part & 15) < 12))
        to, at = iota((128, 384), 0), iota((128, 384), 1)
        same = (to >> 4) == ((at & 127) >> 4)
        widen[...] = one_hot(same & ((at & 15) >= 12) & ((to & 15) == 4 * (at >> 7) + (at & 15) - 12))

    mine, halo = lat.at[pl.ds(2, 2)], lat.at[pl.ds(0, 2)]

    def frame_sum(s, mean):
        def step(i, total):
            v = lat[s, i].astype(F32)
            if mean is not None:
                v = v - mean
                v = v * v
            return total + v

        return jnp.sum(lax.fori_loop(0, 8, step, jnp.zeros((32, C), F32)), axis=0, keepdims=True)

    col = iota((32, C), 0)

    def activate(pair):
        frames = (2 * pair, 2 * pair + 1)
        means = group_means([frame_sum(s, None) for s in frames], gmat[...])
        variances = group_means([frame_sum(s, m) for s, m in zip(frames, means)], gmat[...])
        for s, m, var in zip(frames, means, variances):
            scale = lax.rsqrt(var + 1e-06)
            gain = gain1[...].reshape(1, C)
            empty = (c == 0) & (z < 4) & (q == 0) & (s < 2)

            def step(i, carry):
                v = (lat[s, i].astype(F32) - m) * scale * gain
                v = v / (1.0 + jnp.exp(-v))
                v = jnp.where(empty, 0.0, v)
                at = pl.ds(pl.multiple_of(32 * i + 32, 32), 32)
                act[s, at, 0:C] = jnp.where(col == 0, 0.0, pltpu.roll(v, 1, 0)).astype(BF)
                act[s, at, C : 2 * C] = v.astype(BF)
                act[s, at, 2 * C : 3 * C] = jnp.where(col == 31, 0.0, pltpu.roll(v, 31, 0)).astype(BF)
                return carry

            lax.fori_loop(0, 8, step, 0)

    def taps(ta, frames=(0, 1)):
        t, a = ta // 3, lax.rem(ta, 3)
        for j in frames:
            rows = pl.ds(pl.multiple_of(32 * a, 32), 256)
            acc[j] += dot_nt(act[j + t, rows, :], wall[ta])

    def own_taps(i):
        x3_stage(i)
        taps(near + i)

    def spread(e):
        units = wall[pl.ds(3 * e, 3)].reshape(384, 3 * C)
        wall[7 + e] = dot_nn(widen[...], units).astype(BF)

    q_stage(0)
    constants()
    arrived(gain1, gain_sem.at[0])
    arrived(gain2, gain_sem.at[1])
    relay(0)
    relay(1)
    relay(2)
    relay(3)
    x1_stage(0)
    x1_stage(1)
    q_stage(1)
    x1_stage(2)
    x2_stage(0)
    x1_stage(3)
    q_stage(2)
    x2_stage(1)
    x2_stage(2)
    arrived(mine, lat_sem.at[1])
    send(mine, halo, lat_sem.at[0], sib, z, c == 0)
    for j in range(2):
        acc[j] = dot_nn(lat[2 + j].reshape(256, C), pick[...])
    activate(1)
    x2_stage(3)
    arrived(halo, lat_sem.at[0])
    activate(0)
    own_taps(0)
    q_stage(3)
    own_taps(1)
    own_taps(2)
    own_taps(3)
    spread(c)
    taps(7 + c)

    def sib_unit(n):
        return jnp.where(c == 0, 4 + n, n)

    for n in range(3):
        arrived(wall.at[sib_unit(n)], ssib.at[n])
    spread(1 - c)

    for j in range(2):

        def sib_taps(n, carry):
            taps(jnp.where(n == 3, 8 - c, sib_unit(n)), (j,))
            return carry

        lax.fori_loop(0, 4, sib_taps, 0)
        thr_s[j] = acc[j].astype(BF)
        for k in (j, j + 2):
            dst = thr.at[:, pl.ds(pl.multiple_of(128 * zc, 128), 128)]
            send_or_keep(thr_s.at[j], dst, exsem.at[zc], tm, 4 * g + k)

    q_stage(4)
    for k in range(4):
        arrived(thr.at[:, pl.ds(128 * k, 128)], exsem.at[k])

    through = dot_nn(thr[...], pick_all[...])
    thrn[...] = through

    mean = group_means([jnp.sum(through, axis=0, keepdims=True)], gmat[...])[0]
    dev = through - mean
    var = group_means([jnp.sum(dev * dev, axis=0, keepdims=True)], gmat[...])[0]
    normed = (dev * lax.rsqrt(var + 1e-06) * gain2[...].reshape(1, C)).astype(BF)
    thr[:, 0:C] = normed

    arrived(wq.at[pl.ds(2 * (1 - c), 2)], qsib)
    mine_rows = pl.ds(pl.multiple_of(128 * half, 128), 128)
    queries = dot_nt(thr[mine_rows, 0:C], wq[0]).astype(BF)
    keys = dot_nt(normed, wq[1]).astype(BF)
    values = dot_nt(normed, wq[2]).astype(BF)
    scores = dot_nt(queries, keys) * (C ** -0.5)
    expon = jnp.exp(scores - jnp.max(scores, axis=1, keepdims=True))
    totals = jnp.sum(expon, axis=1, keepdims=True)
    attended = (dot_nn(expon.astype(BF), values) / totals).astype(BF)
    result = thrn[mine_rows, :] + dot_nt(attended, wq[3])
    obuf[...] = result.astype(BF).reshape(4, 32, C)

    fr = 2 * c + fsel
    for k in range(4):
        send_or_keep(obuf.at[k], out_ref.at[fr], outsem.at[fr], 2 * q + g, 4 * half + k)
    for k in range(4):
        arrived(out_ref.at[k], outsem.at[k])

    for when, desc in pending:
        if when is None:
            desc.wait_send()
        else:
            pl.when(when)(desc.wait_send)


def body(latents, gain_one, conv_weight, gain_two, qkv_weight, out_weight):
    c = lax.rem(lax.axis_index("tm"), 2)
    taps = jnp.pad(conv_weight.transpose(2, 0, 1), ((0, 0), (0, 5), (0, 0)))
    proj = jnp.concatenate([qkv_weight.transpose(0, 2, 1), out_weight.T[None]], 0)

    def placed(w):
        low = jnp.pad(w, ((0, 0), (0, 10), (0, 0)))
        high = jnp.pad(w, ((0, 0), (6, 4), (0, 0)))
        return jnp.where(c == 0, low, high)

    vmem = pl.BlockSpec(memory_space=pltpu.VMEM)
    anywhere = pl.BlockSpec(memory_space=pl.ANY)
    dma = pltpu.SemaphoreType.DMA
    out = pl.pallas_call(
        kernel,
        out_shape=jax.ShapeDtypeStruct((4, 32, C), BF),
        in_specs=[anywhere, vmem, vmem, anywhere, anywhere],
        out_specs=vmem,
        scratch_shapes=[
            pltpu.VMEM((4, 8, 32, C), BF),
            pltpu.VMEM((7, 16, 3 * C), BF),
            pltpu.VMEM((4, 16, 3 * C), BF),
            pltpu.VMEM((2, 16, C), BF),
            pltpu.VMEM((4, 16, 3 * C), BF),
            pltpu.VMEM((4, 16, 3 * C), BF),
            pltpu.VMEM((9, 128, 3 * C), BF),
            pltpu.VMEM((2, 64, C), BF),
            pltpu.VMEM((4, C, C), BF),
            pltpu.VMEM((4, 320, 3 * C), BF),
            pltpu.VMEM((2, 256, 128), F32),
            pltpu.VMEM((2, 256, 128), BF),
            pltpu.VMEM((256, 512), BF),
            pltpu.VMEM((256, C), F32),
            pltpu.VMEM((4, 32, C), BF),
            pltpu.VMEM((C, C), BF),
            pltpu.VMEM((C, 128), BF),
            pltpu.VMEM((512, C), BF),
            pltpu.VMEM((128, 384), BF),
            pltpu.VMEM((C,), F32),
            pltpu.VMEM((C,), F32),
            dma((NSEND,)), dma((2,)), dma((5,)), dma((5,)), dma((5,)), dma((5,)), dma((5,)), dma((5,)), dma((5,)),
            dma((4,)), dma((4,)), dma((8,)), dma, dma((4,)), dma((4,)), dma((2,)), dma((5,)),
        ],
        compiler_params=pltpu.CompilerParams(
            collective_id=0, has_side_effects=True, vmem_limit_bytes=40 * 1024 * 1024
        ),
        cost_estimate=pl.CostEstimate(flops=2 * 10**9, bytes_accessed=10**7, transcendentals=10**6),
    )(latents[:, 0], taps, placed(proj), gain_one, gain_two)
    return out[:, None]


def solution(mesh):
    in_specs = (
        P("tm", "rows", None, None),
        P(),
        P(None, None, "tm"),
        P(),
        P(None, None, "tm"),
        P(None, "tm"),
    )
    out_specs = P("tm", "rows", None, None)
    return jax.shard_map(body, mesh=mesh, in_specs=in_specs, out_specs=out_specs, check_vma=False)
```

```python
import jax
import jax.numpy as jnp
from jax import lax
from jax.experimental import pallas as pl
from jax.experimental.pallas import tpu as pltpu
from jax.sharding import PartitionSpec as P

C = 384
NX, NY, NZ = 4, 8, 8
BF = jnp.bfloat16
F32 = jnp.float32
MESH = pl.DeviceIdType.MESH
NSEND = 96


def iota(shape, dim):
    return lax.broadcasted_iota(jnp.int32, shape, dim)


def twelfth(i):
    return (i * 43691) >> 19


def one_hot(mask):
    return jnp.where(mask, 1.0, 0.0).astype(BF)


def dot_nn(a, b):
    return lax.dot_general(a, b, (((1,), (0,)), ((), ())), preferred_element_type=F32)


def dot_nt(a, b):
    return lax.dot_general(a, b, (((1,), (1,)), ((), ())), preferred_element_type=F32)


def group_means(sums, gmat):
    rows = iota((16, C), 0)
    stack = jnp.zeros((16, C), F32)
    for n, s in enumerate(sums):
        high = s.astype(BF).astype(F32)
        rest = s - high
        mid = rest.astype(BF).astype(F32)
        for k, part in enumerate((high, mid, rest - mid)):
            stack = jnp.where(rows == 3 * n + k, part, stack)
    res = dot_nn(stack.astype(BF), gmat)
    out = []
    for n in range(len(sums)):
        total = res[3 * n : 3 * n + 1] + res[3 * n + 1 : 3 * n + 2] + res[3 * n + 2 : 3 * n + 3]
        out.append(total * (1.0 / (12 * 256)))
    return out


def kernel(
    lat_in, wc_in, wq_in, gain1_in, gain2_in, out_ref,
    lat, wc, sibc, sibq, own, mid, wall, qpad, wq, act, acc, thr_s, thr, thrn, obuf, gmat, pick, pick_all, widen, gain1, gain2,
    sends, lat_sem, sibw_sem, yp, ym, xp, xm, xpp, xmm, ssib, qx, qy, qsib, exsem, outsem, gain_sem, mid_sem,
):
    tm = lax.axis_index("tm")
    z = lax.axis_index("rows")
    c = lax.rem(tm, 2)
    q = tm // 2
    x = lax.rem(q, NX)
    y = q // NX
    g = z // 4
    zc = lax.rem(z, 4)
    half = zc // 2
    fsel = lax.rem(zc, 2)

    pending = []

    def place(yy, xx, core):
        return (lax.rem(yy + NY, NY) * NX + lax.rem(xx + NX, NX)) * 2 + core

    def send(src, dst, rsem, to_tm, to_z, when=None):
        d = pltpu.make_async_remote_copy(
            src_ref=src, dst_ref=dst, send_sem=sends.at[len(pending)], recv_sem=rsem,
            device_id=(to_tm, to_z), device_id_type=MESH,
        )
        if when is None:
            d.start()
        else:
            pl.when(when)(d.start)
        pending.append((when, d))

    def send_or_keep(src, dst, rsem, to_tm, to_z):
        here = jnp.logical_and(to_tm == tm, to_z == z)
        send(src, dst, rsem, to_tm, to_z, jnp.logical_not(here))
        pl.when(here)(pltpu.make_async_copy(src, dst, rsem).start)

    def arrived(ref, sem):
        pltpu.make_async_copy(ref, ref, sem).wait()

    for k, (src, dst) in enumerate(((gain1_in, gain1), (gain2_in, gain2))):
        pltpu.make_async_copy(src, dst, gain_sem.at[k]).start()

    def sent(copies):
        for when, desc in copies:
            if when is None:
                desc.wait_send()
            else:
                pl.when(when)(desc.wait_send)

    barrier = pltpu.get_barrier_semaphore()

    def sends_to(c0, z0, c1, z1):
        a = z1 // 4 == c0
        a = a | ((c0 == 0) & (c1 == 0) & (z1 // 4 == 1))
        a = a | (z1 == z0)
        a = a | ((c1 == c0) & (z1 // 4 == z0 // 4))
        a = a | ((c1 == z0 // 4) & (z1 // 4 == lax.rem(z0, 4) // 2))
        return a & jnp.logical_not((c0 == c1) & (z0 == z1))

    def greet(i, count):
        co, zo = i // NZ, lax.rem(i, NZ)

        @pl.when(sends_to(co, zo, c, z))
        def _():
            pl.semaphore_signal(barrier, inc=1, device_id=(2 * q + co, zo), device_id_type=MESH)

        return count + jnp.where(sends_to(c, z, co, zo), 1, 0)

    count = lax.fori_loop(0, 2 * NZ, greet, jnp.int32(0))
    right, left = place(y, x + 1, c), place(y, x - 1, c)
    near_y = [place(y + step, x, c) for step in (1, -1, 2, -2)]
    for other in [right, left] + near_y:
        pl.semaphore_signal(barrier, inc=1, device_id=(other, z), device_id_type=MESH)

    @pl.when(zc == 3)
    def _():
        for step in (3, -3):
            pl.semaphore_signal(barrier, inc=1, device_id=(place(y + step, x, c), z), device_id_type=MESH)

    prev_q = lax.rem(q + 31, 32)

    @pl.when((c == 0) & (z < 4))
    def _():
        def halo_greet(r, carry):
            pl.semaphore_signal(barrier, inc=1, device_id=(2 * prev_q + 1, r), device_id_type=MESH)
            return carry

        lax.fori_loop(0, NZ, halo_greet, 0)

    raw = wc_in[...].reshape(192, C)
    r16, unit = iota((112, 192), 0) & 15, iota((112, 192), 0) >> 4
    third = twelfth(4 * unit)
    tail = r16 >= 12
    chan_of = jnp.where(tail, 4 * (unit - 3 * third) + r16 - 12, r16)
    tap_row = jnp.where(tail, 7 + third, unit)
    shard_row, tap = iota((112, 192), 1) >> 5, iota((112, 192), 1) & 31
    for b in range(3):
        wanted = (chan_of == 6 * c + shard_row) & (tap == 3 * tap_row + b) & (tap_row < 9)
        wc[:, :, b * C : (b + 1) * C] = dot_nn(one_hot(wanted), raw).astype(BF).reshape(7, 16, C)

    pl.semaphore_wait(barrier, count + 6 + 4 * c + jnp.where(zc == 3, 2, 0))

    sib = 2 * q + 1 - c
    far_row = jnp.where(zc == 0, 4, -zc)

    near, far = 3 * c, 3 * (1 - c)
    send(wc.at[pl.ds(far, 4)], sibc, sibw_sem.at[0], sib, z)
    send(wq_in.at[pl.ds(2 * (1 - c), 2)], sibq, sibw_sem.at[1], sib, z)

    q_halo = lax.rem(q + c, 32)
    for k in range(4):
        send_or_keep(lat_in.at[pl.ds(0, 2)], lat.at[pl.ds(2, 2), z], lat_sem.at[1], 2 * q, 4 * c + k)
        send_or_keep(lat_in.at[pl.ds(2, 2)], lat.at[pl.ds(2, 2), z], lat_sem.at[1], 2 * q + 1, 4 * c + k)
        send_or_keep(lat_in.at[pl.ds(2, 2)], lat.at[pl.ds(0, 2), z], lat_sem.at[0], 2 * q_halo, 4 * (1 - c) + k)

    def rows_of(slot, n=1):
        return pl.ds(pl.multiple_of(16 * slot, 16), 16 * n)

    kinds = pl.ds(2 * c, 2)

    def wpart(i, slot, n=1):
        return wall.at[near + i, rows_of(slot, n), :]

    def post(src, rsem, to_tm, index):
        return pltpu.make_async_remote_copy(
            src_ref=src, dst_ref=src, send_sem=sends.at[index], recv_sem=rsem,
            device_id=(to_tm, z), device_id_type=MESH,
        )

    to_first, to_second = place(y - zc, x, c), place(y - far_row, x, c)
    arrived(sibc, sibw_sem.at[0])
    for i in range(4):
        own[i] = wc[near + i] + sibc[i]
        for h, (to, sem) in enumerate(((to_first, yp), (to_second, ym))):
            copy = pltpu.make_async_remote_copy(
                src_ref=own.at[i], dst_ref=wpart(i, 2 * x + h), send_sem=sends.at[len(pending)],
                recv_sem=sem.at[i], device_id=(to, z), device_id_type=MESH,
            )
            pl.when(zc != 0)(copy.start)
            pending.append((zc != 0, copy))

    hops = []
    for i in range(4):
        for src, dst, sem in ((own.at[i], mid.at[i], mid_sem), (mid.at[i], wpart(i, 2 * x + 1), ym)):
            copy = pltpu.make_async_remote_copy(
                src_ref=src, dst_ref=dst, send_sem=sends.at[len(pending)], recv_sem=sem.at[i],
                device_id=(near_y[2 + i % 2], z), device_id_type=MESH,
            )
            pending.append((zc == 0, copy))
            hops.append(copy)

    @pl.when(zc == 0)
    def _():
        for i in range(4):
            hops[2 * i].start()

    def relay(i):
        @pl.when(zc == 0)
        def _():
            arrived(mid.at[i], mid_sem.at[i])
            hops[2 * i + 1].start()

    arrived(sibq, sibw_sem.at[1])
    for k in range(2):
        qpad[k, rows_of(x), :] = wq_in[2 * c + k] + sibq[k]

    xl, xr, xo = lax.rem(x + 3, 4), lax.rem(x + 1, 4), lax.rem(x + 2, 4)

    first_x = len(pending)
    rights = [post(wpart(i, 2 * x, 2), xp.at[i], right, first_x + i) for i in range(4)]
    lefts = [post(wpart(i, 2 * x, 2), xm.at[i], left, first_x + 4 + i) for i in range(4)]
    pending.extend((None, copy) for copy in rights + lefts)

    def x1_stage(i):
        @pl.when(zc == 0)
        def _():
            wall[near + i, rows_of(2 * x), :] = own[i]

        @pl.when(zc != 0)
        def _():
            arrived(wpart(i, 2 * x), yp.at[i])

        arrived(wpart(i, 2 * x + 1), ym.at[i])
        rights[i].start()
        lefts[i].start()

    def x2_stage(i):
        arrived(wpart(i, 2 * xl, 2), xp.at[i])
        send(wpart(i, 2 * xl), wpart(i, 2 * xl), xpp.at[i], right, z)
        arrived(wpart(i, 2 * xr, 2), xm.at[i])
        send(wpart(i, 2 * xr + 1), wpart(i, 2 * xr + 1), xmm.at[i], left, z)

    def x3_stage(i):
        arrived(wpart(i, 2 * xo), xpp.at[i])
        arrived(wpart(i, 2 * xo + 1), xmm.at[i])
        n = jnp.where(c == 0, i, i - 1)
        whole = wall.at[near + i]
        when = None if 0 < i < 3 else (c == 0 if i == 0 else c == 1)
        n = jnp.clip(n, 0, 2)
        send(whole, whole, ssib.at[n], sib, z, when)

    def xpart(k, nk, xx):
        return qpad.at[pl.ds(k, nk), rows_of(xx), :]

    def ypart(k, nk, step):
        yy = lax.rem(y + 8 + step, 8)
        return wq.at[pl.ds(2 * c + k, nk), pl.ds(pl.multiple_of(48 * yy, 16), 48), :]

    def q_stage(s):
        if s == 0:
            piece = xpart(0, 2, x)
            send(piece, piece, qx.at[0], right, z)
            send(piece, piece, qx.at[1], left, z)
        elif s == 1:
            arrived(xpart(0, 2, xl), qx.at[0])
            part = xpart(0, 1, xl)
            send(part, part, qx.at[2], right, z)
            arrived(xpart(0, 2, xr), qx.at[1])
            part = xpart(1, 1, xr)
            send(part, part, qx.at[3], left, z)
        elif s == 2:
            arrived(xpart(0, 1, xo), qx.at[2])
            arrived(xpart(1, 1, xo), qx.at[3])
            wide = iota((48, 64), 0)
            tight = one_hot(iota((48, 64), 1) == wide + 4 * twelfth(wide))
            for k in range(2):
                wq[2 * c + k, pl.ds(pl.multiple_of(48 * y, 16), 48), :] = dot_nn(tight, qpad[k]).astype(BF)
            block = ypart(0, 2, 0)
            for n in range(4):
                send(block, block, qy.at[n], near_y[n], z)
        elif s == 3:
            for n, step in enumerate((-1, 1, -2, 2)):
                arrived(ypart(0, 2, step), qy.at[n])
            for n, (step, k, nk) in enumerate(((-1, 0, 2), (1, 0, 2), (-2, 0, 1), (2, 1, 1))):
                block = ypart(k, nk, step)
                send(block, block, qy.at[4 + n], near_y[2 + n % 2], z)
        else:
            for n, (step, k, nk) in enumerate(((-3, 0, 2), (3, 0, 2), (4, 0, 1), (4, 1, 1))):
                arrived(ypart(k, nk, step), qy.at[4 + n])
            both = wq.at[kinds]
            send(both, both, qsib, sib, z)

    def constants():
        gmat[...] = one_hot(twelfth(iota((C, C), 0)) == twelfth(iota((C, C), 1)))
        zero = jnp.zeros((32, 3 * C), BF)
        for s in range(4):
            act[s, 0:32, :] = zero
            act[s, 288:320, :] = zero
        def channel(place_in, k):
            slot = (place_in & 127) >> 4
            row_of = (y + 8 + jnp.where((slot & 1) == 0, k, jnp.where(k == 0, 4, -k))) & 7
            return 12 * (row_of * 4 + (slot >> 1)) + (place_in & 15)

        lane = iota((C, 128), 1)
        chan = channel(lane, zc)
        pick[...] = one_hot((iota((C, 128), 0) == chan) & ((lane & 15) < 12))
        part = iota((512, C), 0)
        chan = channel(part, part >> 7)
        pick_all[...] = one_hot((iota((512, C), 1) == chan) & ((part & 15) < 12))
        to, at = iota((128, 384), 0), iota((128, 384), 1)
        same = (to >> 4) == ((at & 127) >> 4)
        widen[...] = one_hot(same & ((at & 15) >= 12) & ((to & 15) == 4 * (at >> 7) + (at & 15) - 12))

    mine, halo = lat.at[pl.ds(2, 2)], lat.at[pl.ds(0, 2)]

    def frame_sum(s, mean):
        def step(i, total):
            v = lat[s, i].astype(F32)
            if mean is not None:
                v = v - mean
                v = v * v
            return total + v

        return jnp.sum(lax.fori_loop(0, 8, step, jnp.zeros((32, C), F32)), axis=0, keepdims=True)

    col = iota((32, C), 0)

    def activate(pair):
        frames = (2 * pair, 2 * pair + 1)
        means = group_means([frame_sum(s, None) for s in frames], gmat[...])
        variances = group_means([frame_sum(s, m) for s, m in zip(frames, means)], gmat[...])
        for s, m, var in zip(frames, means, variances):
            scale = lax.rsqrt(var + 1e-06)
            gain = gain1[...].reshape(1, C)
            empty = (c == 0) & (z < 4) & (q == 0) & (s < 2)

            def step(i, carry):
                v = (lat[s, i].astype(F32) - m) * scale * gain
                v = v / (1.0 + jnp.exp(-v))
                v = jnp.where(empty, 0.0, v)
                at = pl.ds(pl.multiple_of(32 * i + 32, 32), 32)
                act[s, at, 0:C] = jnp.where(col == 0, 0.0, pltpu.roll(v, 1, 0)).astype(BF)
                act[s, at, C : 2 * C] = v.astype(BF)
                act[s, at, 2 * C : 3 * C] = jnp.where(col == 31, 0.0, pltpu.roll(v, 31, 0)).astype(BF)
                return carry

            lax.fori_loop(0, 8, step, 0)

    def taps(ta, frames=(0, 1)):
        t, a = ta // 3, lax.rem(ta, 3)
        for j in frames:
            rows = pl.ds(pl.multiple_of(32 * a, 32), 256)
            acc[j] += dot_nt(act[j + t, rows, :], wall[ta])

    def own_taps(i):
        x3_stage(i)
        taps(near + i)

    def spread(e):
        units = wall[pl.ds(3 * e, 3)].reshape(384, 3 * C)
        wall[7 + e] = dot_nn(widen[...], units).astype(BF)

    q_stage(0)
    constants()
    arrived(gain1, gain_sem.at[0])
    arrived(gain2, gain_sem.at[1])
    relay(0)
    relay(1)
    relay(2)
    relay(3)
    x1_stage(0)
    x1_stage(1)
    q_stage(1)
    x1_stage(2)
    x2_stage(0)
    x1_stage(3)
    q_stage(2)
    x2_stage(1)
    x2_stage(2)
    arrived(mine, lat_sem.at[1])
    send(mine, halo, lat_sem.at[0], sib, z, c == 0)
    for j in range(2):
        acc[j] = dot_nn(lat[2 + j].reshape(256, C), pick[...])
    activate(1)
    x2_stage(3)
    arrived(halo, lat_sem.at[0])
    activate(0)
    own_taps(0)
    q_stage(3)
    own_taps(1)
    own_taps(2)
    own_taps(3)
    spread(c)
    taps(7 + c)

    def sib_unit(n):
        return jnp.where(c == 0, 4 + n, n)

    for n in range(3):
        arrived(wall.at[sib_unit(n)], ssib.at[n])
    spread(1 - c)

    early = len(pending)

    for j in range(2):

        def sib_taps(n, carry):
            taps(jnp.where(n == 3, 8 - c, sib_unit(n)), (j,))
            return carry

        lax.fori_loop(0, 4, sib_taps, 0)
        thr_s[j] = acc[j].astype(BF)
        for k in (j, j + 2):
            dst = thr.at[:, pl.ds(pl.multiple_of(128 * zc, 128), 128)]
            send_or_keep(thr_s.at[j], dst, exsem.at[zc], tm, 4 * g + k)

    q_stage(4)
    sent(pending[:early])
    for k in range(4):
        arrived(thr.at[:, pl.ds(128 * k, 128)], exsem.at[k])

    through = dot_nn(thr[...], pick_all[...])
    thrn[...] = through

    mean = group_means([jnp.sum(through, axis=0, keepdims=True)], gmat[...])[0]
    dev = through - mean
    var = group_means([jnp.sum(dev * dev, axis=0, keepdims=True)], gmat[...])[0]
    normed = (dev * lax.rsqrt(var + 1e-06) * gain2[...].reshape(1, C)).astype(BF)
    thr[:, 0:C] = normed

    arrived(wq.at[pl.ds(2 * (1 - c), 2)], qsib)
    mine_rows = pl.ds(pl.multiple_of(128 * half, 128), 128)
    queries = dot_nt(thr[mine_rows, 0:C], wq[0]).astype(BF)
    keys = dot_nt(normed, wq[1]).astype(BF)
    values = dot_nt(normed, wq[2]).astype(BF)
    scores = dot_nt(queries, keys) * (C ** -0.5)
    expon = jnp.exp(scores - jnp.max(scores, axis=1, keepdims=True))
    totals = jnp.sum(expon, axis=1, keepdims=True)
    attended = (dot_nn(expon.astype(BF), values) / totals).astype(BF)
    result = thrn[mine_rows, :] + dot_nt(attended, wq[3])
    obuf[...] = result.astype(BF).reshape(4, 32, C)

    fr = 2 * c + fsel
    for k in range(4):
        send_or_keep(obuf.at[k], out_ref.at[fr], outsem.at[fr], 2 * q + g, 4 * half + k)
    for k in range(4):
        arrived(out_ref.at[k], outsem.at[k])

    sent(pending[early:])


def body(latents, gain_one, conv_weight, gain_two, qkv_weight, out_weight):
    c = lax.rem(lax.axis_index("tm"), 2)
    taps = jnp.pad(conv_weight.transpose(2, 0, 1), ((0, 0), (0, 5), (0, 0)))
    proj = jnp.concatenate([qkv_weight.transpose(0, 2, 1), out_weight.T[None]], 0)

    def placed(w):
        low = jnp.pad(w, ((0, 0), (0, 10), (0, 0)))
        high = jnp.pad(w, ((0, 0), (6, 4), (0, 0)))
        return jnp.where(c == 0, low, high)

    vmem = pl.BlockSpec(memory_space=pltpu.VMEM)
    anywhere = pl.BlockSpec(memory_space=pl.ANY)
    dma = pltpu.SemaphoreType.DMA
    out = pl.pallas_call(
        kernel,
        out_shape=jax.ShapeDtypeStruct((4, 32, C), BF),
        in_specs=[anywhere, vmem, vmem, anywhere, anywhere],
        out_specs=vmem,
        scratch_shapes=[
            pltpu.VMEM((4, 8, 32, C), BF),
            pltpu.VMEM((7, 16, 3 * C), BF),
            pltpu.VMEM((4, 16, 3 * C), BF),
            pltpu.VMEM((2, 16, C), BF),
            pltpu.VMEM((4, 16, 3 * C), BF),
            pltpu.VMEM((4, 16, 3 * C), BF),
            pltpu.VMEM((9, 128, 3 * C), BF),
            pltpu.VMEM((2, 64, C), BF),
            pltpu.VMEM((4, C, C), BF),
            pltpu.VMEM((4, 320, 3 * C), BF),
            pltpu.VMEM((2, 256, 128), F32),
            pltpu.VMEM((2, 256, 128), BF),
            pltpu.VMEM((256, 512), BF),
            pltpu.VMEM((256, C), F32),
            pltpu.VMEM((4, 32, C), BF),
            pltpu.VMEM((C, C), BF),
            pltpu.VMEM((C, 128), BF),
            pltpu.VMEM((512, C), BF),
            pltpu.VMEM((128, 384), BF),
            pltpu.VMEM((C,), F32),
            pltpu.VMEM((C,), F32),
            dma((NSEND,)), dma((2,)), dma((2,)), dma((5,)), dma((5,)), dma((5,)), dma((5,)), dma((5,)), dma((5,)),
            dma((4,)), dma((4,)), dma((8,)), dma, dma((4,)), dma((4,)), dma((2,)), dma((5,)),
        ],
        compiler_params=pltpu.CompilerParams(
            collective_id=0, has_side_effects=True, vmem_limit_bytes=40 * 1024 * 1024
        ),
        cost_estimate=pl.CostEstimate(flops=2 * 10**9, bytes_accessed=10**7, transcendentals=10**6),
    )(latents[:, 0], taps, placed(proj), gain_one, gain_two)
    return out[:, None]


def solution(mesh):
    in_specs = (
        P("tm", "rows", None, None),
        P(),
        P(None, None, "tm"),
        P(),
        P(None, None, "tm"),
        P(None, "tm"),
    )
    out_specs = P("tm", "rows", None, None)
    return jax.shard_map(body, mesh=mesh, in_specs=in_specs, out_specs=out_specs, check_vma=False)
```
